32 devices in a mesh: ctx: 16 (over z, y, core), rep: 2 (over x).
Axes of the slice: x: 2, y: 2, z: 4, core: 2. Of those that a mesh axis runs over, the one named last changes fastest.
Arguments:
- tokens: bfloat16 [4096, 8192], P('ctx'), may hold values from -6 to 6
- norm_gain: bfloat16 [8192], replicated, may hold values from 0.099609375 to 1.8984375
- q_weight: bfloat16 [8192, 4096], P('ctx', 'rep'), may hold values from -0.0625 to 0.0625
- q_bias: bfloat16 [4096], P('rep'), may hold values from -48 to 48
- key_value_weight: bfloat16 [8192, 1024], P('ctx', 'rep'), may hold values from -0.0625 to 0.0625
- kv_bias: bfloat16 [1024], P('rep'), may hold values from -8 to 8
- out_weight: bfloat16 [4096, 8192], P('rep', 'ctx'), may hold values from -0.5 to 0.5
Outputs:
- attn_out: bfloat16 [4096, 8192], P(('ctx', 'rep'))
- key_value_cache: bfloat16 [4096, 1024], P('ctx')
The draws below stay inside these ranges and needn't reach their ends.
All inputs are finite; a program needn't handle non-finite values.
Results may differ from the reference program's by a relative error of at most 0.014.
The reference program's roundings to bfloat16 on the way count: a program that leaves them out, or rounds other values in their place, can miss the bound.
Values may be sent and summed in bfloat16 or wider, within the bound.
No kernel may reach another device: no remote copies, remote signals or barrier semaphores. Data moves between devices by JAX's collectives and lax.ppermute only.
A program may use at most 128 MiB of HBM per device.

```python
import jax
import jax.numpy as jnp
from jax import lax

MODEL_WIDTH = 8192
HEAD_SIZE = 128
QUERY_HEADS = 32
KEY_VALUE_HEADS = 4
PREFIX_TOKENS = 4096
N_REP = 2


def bias_parts(key):
    key_offset_bias = jax.random.normal(jax.random.fold_in(key, 11), (KEY_VALUE_HEADS, HEAD_SIZE), jnp.float32)
    value_offset_bias = 0.5 * jax.random.normal(jax.random.fold_in(key, 12), (KEY_VALUE_HEADS * HEAD_SIZE,), jnp.float32)
    random_jitter = jax.random.normal(jax.random.fold_in(key, 14), (QUERY_HEADS, HEAD_SIZE), jnp.float32)
    key_offset_bias = 0.5 * key_offset_bias
    query_offset_bias = 0.5 * random_jitter
    return (query_offset_bias.reshape(-1), jnp.concatenate([key_offset_bias.reshape(-1), value_offset_bias]))


def draw_q_bias(key, part):
    query_offset_bias, other = bias_parts(key)
    return jnp.clip(query_offset_bias, -48.0, 48.0).astype(jnp.bfloat16)


def draw_kv_bias(key, part):
    other, kv_part = bias_parts(key)
    return jnp.clip(kv_part, -8.0, 8.0).astype(jnp.bfloat16)


def level_of(stream_key, extent, cuts, least, top_value):
    gain = 1.0
    for position, blocks in cuts:
        draws = jax.random.uniform(jax.random.fold_in(jax.random.fold_in(stream_key, 6), position), (blocks,), jnp.float32, least / len(cuts), top_value / len(cuts))
        gain = gain * jnp.repeat(jnp.exp(draws), extent[position] // blocks).reshape((-1,) + (1,) * (len(extent) - 1 - position))
    return gain


def normal_values(key, dims, spread, limit, cuts=(), held_as=jnp.bfloat16):
    factor_of = level_of(key, dims, cuts, -0.22, 0.18) if cuts else 1.0
    drawn = jax.random.normal(key, dims, jnp.float32) * spread * factor_of
    return jnp.minimum(jnp.maximum(drawn, -limit), limit).astype(held_as)


def setup_inputs(seed: int = 0) -> dict:
    key_of = jax.random.split(jax.random.key(seed), 8)
    return {
        "tokens": normal_values(key_of[0], (PREFIX_TOKENS, MODEL_WIDTH), 1.0, 6.0, ((0, 16),)),
        "norm_gain": jnp.clip(1.0 + 0.18 * jax.random.normal(key_of[1], (MODEL_WIDTH,), jnp.float32), 0.099609375, 1.8984375).astype(jnp.bfloat16),
        "q_weight": normal_values(key_of[2], (MODEL_WIDTH, QUERY_HEADS * HEAD_SIZE), MODEL_WIDTH ** -0.5, 0.0625, ((0, 16), (1, 2))),
        "q_bias": draw_q_bias(jax.random.fold_in(key_of[7], 71), 0),
        "key_value_weight": normal_values(key_of[4], (MODEL_WIDTH, 2 * KEY_VALUE_HEADS * HEAD_SIZE), MODEL_WIDTH ** -0.5, 0.0625, ((0, 16), (1, 2))),
        "kv_bias": draw_kv_bias(jax.random.fold_in(key_of[7], 71), 0),
        "out_weight": normal_values(key_of[6], (QUERY_HEADS * HEAD_SIZE, MODEL_WIDTH), HEAD_SIZE ** -0.5, 0.5, ((0, 2), (1, 16))),
    }


rope_base = 1000000.0

def apply_rotation(value_rows, token_positions):
    middle = value_rows.shape[-1] // 2
    exponent = jnp.arange(middle, dtype=jnp.float32) * (2.0 / value_rows.shape[-1])
    inverse = rope_base ** (-exponent)
    angles = token_positions.astype(jnp.float32)[:, None] * inverse[None, :]
    cosine = jnp.cos(angles)[:, None, :]
    sine_part = jnp.sin(angles)[:, None, :]
    leading = value_rows[..., :middle]
    trailing = value_rows[..., middle:]
    return jnp.concatenate([leading * cosine - trailing * sine_part, trailing * cosine + leading * sine_part], axis=-1)

def reference(tokens, norm_gain, q_weight, q_bias, key_value_weight, kv_bias, out_weight):
    values_in = tokens.astype(jnp.float32)
    scale_row = lax.rsqrt(lax.optimization_barrier(jnp.mean(values_in * values_in, axis=-1, keepdims=True)) + 1e-06)
    normed = (values_in * scale_row * norm_gain.astype(jnp.float32)).astype(jnp.bfloat16)
    token_positions = jnp.arange(PREFIX_TOKENS, dtype=jnp.int32)
    query_sum = jnp.dot(normed, q_weight, preferred_element_type=jnp.float32) + q_bias.astype(jnp.float32)
    query_rows = apply_rotation(query_sum.reshape(PREFIX_TOKENS, QUERY_HEADS, HEAD_SIZE), token_positions).astype(jnp.bfloat16)
    key_value_sum = jnp.dot(normed, key_value_weight, preferred_element_type=jnp.float32) + kv_bias.astype(jnp.float32)
    key_section = apply_rotation(key_value_sum[:, :KEY_VALUE_HEADS * HEAD_SIZE].reshape(PREFIX_TOKENS, KEY_VALUE_HEADS, HEAD_SIZE), token_positions).reshape(PREFIX_TOKENS, KEY_VALUE_HEADS * HEAD_SIZE)
    key_value_cache = jnp.concatenate([key_section, key_value_sum[:, KEY_VALUE_HEADS * HEAD_SIZE:]], axis=1).astype(jnp.bfloat16)
    key_rows = key_value_cache[:, :KEY_VALUE_HEADS * HEAD_SIZE].reshape(PREFIX_TOKENS, KEY_VALUE_HEADS, HEAD_SIZE).astype(jnp.float32)
    value_rows = key_value_cache[:, KEY_VALUE_HEADS * HEAD_SIZE:].reshape(PREFIX_TOKENS, KEY_VALUE_HEADS, HEAD_SIZE).astype(jnp.float32)
    head_group = QUERY_HEADS // KEY_VALUE_HEADS
    grouped_rows = query_rows.reshape(PREFIX_TOKENS, KEY_VALUE_HEADS, head_group, HEAD_SIZE).astype(jnp.float32)
    block = min(512, PREFIX_TOKENS)
    pieces = []
    for index in range(PREFIX_TOKENS // block):
        finish = (index + 1) * block
        query_block = grouped_rows[index * block:finish]
        scores = jnp.einsum('rgjd,pgd->gjrp', query_block, key_rows[:finish]) * HEAD_SIZE ** (-0.5)
        query_pos = jnp.arange(index * block, finish, dtype=jnp.int32)
        key_pos = jnp.arange(finish, dtype=jnp.int32)
        allowed = key_pos[None, :] <= query_pos[:, None]
        scores = jnp.where(allowed, scores, -1e+30)
        maximum = lax.optimization_barrier(jnp.max(scores, axis=-1, keepdims=True))
        expo = jnp.where(allowed, jnp.exp(scores - maximum), 0.0)
        total = lax.optimization_barrier(jnp.sum(expo, axis=-1))
        weights = expo.astype(jnp.bfloat16).astype(jnp.float32)
        summed = jnp.einsum('gjrp,pgd->gjrd', weights, value_rows[:finish])
        result = summed / total[..., None]
        pieces.append(jnp.transpose(result, (2, 0, 1, 3)).reshape(block, QUERY_HEADS * HEAD_SIZE).astype(jnp.bfloat16))
    attended = jnp.concatenate(pieces, axis=0)
    width = QUERY_HEADS * HEAD_SIZE // N_REP
    accum = jnp.zeros((PREFIX_TOKENS, MODEL_WIDTH), jnp.float32)
    for member in range(N_REP):
        partial_value = jnp.dot(attended[:, member * width:(member + 1) * width], out_weight[member * width:(member + 1) * width], preferred_element_type=jnp.float32)
        rounded = lax.optimization_barrier(partial_value.astype(jnp.bfloat16))
        accum = accum + rounded.astype(jnp.float32)
    return (accum.astype(jnp.bfloat16), key_value_cache)
```

```python
import functools

import jax
import jax.numpy as jnp
from jax import lax
from jax.experimental import pallas as pl
from jax.experimental.pallas import tpu as pltpu
from jax.sharding import PartitionSpec as P

HEAD_SIZE = 128
QUERY_HEADS = 32
KEY_VALUE_HEADS = 4
ROPE_BASE = 1000000.0
CORE, Y, SPLIT = 1, 2, 4
VMEM_LIMIT = 48 * 1024 * 1024
LOG2E = 1.4426950408889634
VM = pl.BlockSpec(memory_space=pltpu.VMEM)
SM = pl.BlockSpec(memory_space=pltpu.SMEM)


def swap(x, mask):
    n = lax.axis_size("ctx")
    return lax.ppermute(x, "ctx", [(i, i ^ mask) for i in range(n)])


def swap_rep(x, mask):
    n = lax.axis_size("rep")
    return lax.ppermute(x, "rep", [(i, i ^ mask) for i in range(n)])


def after(x, *tokens):
    tokens = tuple(t for t in tokens if t is not None)
    if not tokens:
        return x
    return lax.optimization_barrier((x,) + tokens)[0]


def gather_rep(x, axis):
    rep = lax.axis_index("rep")
    bit = 1
    while bit < lax.axis_size("rep"):
        other = swap_rep(x, bit)
        high = (rep & bit) != 0
        x = jnp.concatenate([jnp.where(high, other, x), jnp.where(high, x, other)], axis=axis)
        bit *= 2
    return x


def call(body, out_shape, specs, flops, nbytes, args, scratch=(), name=None):
    outs = tuple(out_shape)
    return pl.pallas_call(
        body,
        out_shape=outs,
        in_specs=specs,
        out_specs=tuple(VM for _ in outs),
        scratch_shapes=list(scratch),
        compiler_params=pltpu.CompilerParams(vmem_limit_bytes=VMEM_LIMIT),
        cost_estimate=pl.CostEstimate(flops=flops, bytes_accessed=nbytes, transcendentals=0),
        name=name,
    )(*args)


def norm_body(masks, place, tokens, gain, own, send):
    ctx = place[0]
    rows, width = tokens.shape
    kb = own.shape[1] // len(masks)
    step = 32

    def chunk(i, carry):
        part = pl.ds(i * step, step)
        t = tokens[part, :].astype(jnp.float32)
        scale = lax.rsqrt(jnp.sum(t * t, axis=-1, keepdims=True) * (1.0 / width) + 1e-06)
        for extra, ref in ((0, own), (SPLIT, send)):
            for j, m in enumerate(masks):
                block = pl.ds(pl.multiple_of((ctx ^ (m | extra)) * kb, 128), kb)
                v = tokens[part, block].astype(jnp.float32) * scale * gain[:, block].astype(jnp.float32)
                ref[part, j * kb : (j + 1) * kb] = v.astype(jnp.bfloat16)
        return carry

    lax.fori_loop(0, rows // step, chunk, 0)


def project_body(a_own, a_recv, *refs):
    weights, outs = refs[:-2], refs[-2:]
    kb = weights[0].shape[0]
    for a, out in zip((a_own, a_recv), outs):
        total = None
        for j, w in enumerate(weights):
            part = jnp.dot(a[:, j * kb : (j + 1) * kb], w[...], preferred_element_type=jnp.float32)
            total = part if total is None else total + part
        out[...] = total.astype(out.dtype)


def rotate(v, cosine, sine):
    half = HEAD_SIZE // 2
    turned = jnp.concatenate([v[:, half:], v[:, :half]], axis=1)
    return v * cosine + turned * sine


def attend_body(n_bits, place, mine, other, bias, cosine, sine, keys, values, out, q, acc, top, total):
    ctx = place[0]
    rows, width = mine.shape
    heads = width // HEAD_SIZE
    for h in range(heads):
        cols = slice(h * HEAD_SIZE, (h + 1) * HEAD_SIZE)
        v = mine[:, cols] + other[:, cols].astype(jnp.float32) + bias[:, cols].astype(jnp.float32)
        q[h * rows : (h + 1) * rows, :] = rotate(v, cosine[...], sine[...]).astype(jnp.bfloat16)
    factor = LOG2E * HEAD_SIZE ** (-0.5)

    def scores(pos):
        k = keys[pl.ds(pl.multiple_of(pos * rows, 128), rows), :]
        return lax.dot_general(q[...], k, (((1,), (1,)), ((), ())), preferred_element_type=jnp.float32)

    def weighted(p, pos):
        v = values[pl.ds(pl.multiple_of(pos * rows, 128), rows), :]
        return jnp.dot(p.astype(jnp.bfloat16), v, preferred_element_type=jnp.float32)

    s = scores(0)
    r = lax.broadcasted_iota(jnp.int32, s.shape, 0) % rows
    c = lax.broadcasted_iota(jnp.int32, s.shape, 1)
    s = jnp.where(c <= r, s, -1e30)
    m = jnp.max(s, axis=-1, keepdims=True)
    p = jnp.exp2((s - m) * factor)
    top[...] = m
    total[...] = jnp.sum(p, axis=-1, keepdims=True)
    acc[...] = weighted(p, 0)

    def block(b, carry):
        k = ctx ^ b
        pos = (k >> 2) | ((k & 2) << (n_bits - 3)) | ((k & 1) << (n_bits - 1))
        s = scores(pos)
        old = top[...]
        m = jnp.maximum(old, jnp.max(s, axis=-1, keepdims=True))
        p = jnp.exp2((s - m) * factor)
        shrink = jnp.exp2((old - m) * factor)
        top[...] = m
        total[...] = total[...] * shrink + jnp.sum(p, axis=-1, keepdims=True)
        acc[...] = acc[...] * shrink + weighted(p, pos)
        return carry

    lax.fori_loop(0, ctx, block, 0)
    result = acc[...] / total[...]
    for h in range(heads):
        out[:, h * HEAD_SIZE : (h + 1) * HEAD_SIZE] = result[h * rows : (h + 1) * rows].astype(jnp.bfloat16)


def output_body(n_att, place, *refs):
    own, recv = refs[:n_att], refs[n_att : 2 * n_att]
    weights, outs = refs[2 * n_att : -1], refs[-1]
    rep = place[1]
    rows = own[0].shape[0]
    members = outs.shape[0]
    size = rows // members
    wide = own[0].shape[1]
    n = weights[0].shape[1]
    for far in range(members):
        part = pl.ds(pl.multiple_of((rep ^ far) * size, size), size)
        for i, att in enumerate((own, recv)):
            for j, w in enumerate(weights):
                total = None
                for a, piece in enumerate(att):
                    term = jnp.dot(piece[part, :], w[a * wide : (a + 1) * wide, :], preferred_element_type=jnp.float32)
                    total = term if total is None else total + term
                outs[far, i * size : (i + 1) * size, j * n : (j + 1) * n] = total.astype(jnp.bfloat16)


def place_body(masks, n_sub, place, *refs):
    own, recv, out = refs[:n_sub], refs[n_sub:-1], refs[-1]
    ctx = place[0]
    sub = own[0].shape[1] // len(masks)
    block = sub * n_sub
    for extra, group in ((0, own), (SPLIT, recv)):
        for s, ref in enumerate(group):
            for j, m in enumerate(masks):
                start = (ctx ^ (m | extra)) * block + s * sub
                out[:, pl.ds(pl.multiple_of(start, 128), sub)] = ref[:, j * sub : (j + 1) * sub]


def per_device(tokens, norm_gain, q_weight, q_bias, kv_weight, kv_bias, out_weight):
    rows, width = tokens.shape
    n_ctx, n_rep = lax.axis_size("ctx"), lax.axis_size("rep")
    n_bits = n_ctx.bit_length() - 1
    ctx, rep = lax.axis_index("ctx"), lax.axis_index("rep")
    place = jnp.stack([ctx, rep]).astype(jnp.int32)
    head_group = QUERY_HEADS // KEY_VALUE_HEADS
    local_heads = q_weight.shape[1] // HEAD_SIZE
    kv_heads = max(1, local_heads // head_group)
    high_bits = [1 << b for b in range(3, n_bits)]
    masks = [0]
    for bit in high_bits + [Y, CORE]:
        masks = masks + [m | bit for m in masks]
    masks = sorted(masks)
    n_masks = len(masks)

    n_q = min(4, local_heads)
    q_cols = q_weight.shape[1] // n_q
    n_out = max(1, min(4, out_weight.shape[1] // 128))
    out_cols = out_weight.shape[1] // n_out
    pieces = [kv_weight]
    pieces += [q_weight[:, i * q_cols : (i + 1) * q_cols] for i in range(n_q)]
    pieces += [out_weight[:, i * out_cols : (i + 1) * out_cols] for i in range(n_out)]
    high_done, y_done = [], []
    gathered = []
    firsts = []
    for i, piece in enumerate(pieces):
        blocks = {0: piece}
        for bit in high_bits:
            for m in list(blocks):
                got = swap(after(blocks[m], *high_done[-2:-1]), bit)
                high_done.append(got)
                blocks[m | bit] = got
        firsts.append(blocks)
    order = []
    for i in range(len(pieces) + 1):
        if i < len(pieces):
            order.append((i, 0))
        if i > 0:
            order += [(i - 1, m) for m in sorted(firsts[i - 1]) if m]
    for i, m in order:
        got = swap(after(firsts[i][m], *y_done[-2:-1]), Y)
        y_done.append(got)
        firsts[i][m | Y] = got
    for blocks in firsts:
        for m in list(blocks):
            blocks[m | CORE] = swap(blocks[m], CORE)
        gathered.append([blocks[m] for m in masks])

    half = width // 2
    wide = jax.ShapeDtypeStruct((rows, half), jnp.bfloat16)
    a_own, a_send = call(
        functools.partial(norm_body, masks), (wide, wide), [SM, VM, VM], 0, 3 * rows * width * 2,
        (place, tokens, norm_gain.reshape(1, width)), name="normed",
    )
    a_part = lax.dynamic_slice_in_dim(a_send, rep * (rows // n_rep), rows // n_rep, 0)
    a_recv = gather_rep(swap(a_part, SPLIT), 0)

    def project(weights, name):
        n = weights[0].shape[1]
        kept, sent = call(
            project_body,
            (jax.ShapeDtypeStruct((rows, n), jnp.float32), jax.ShapeDtypeStruct((rows, n), jnp.bfloat16)),
            [VM] * (2 + n_masks), 2 * 2 * rows * half * n, 2 * rows * half * 2 + half * n * 2,
            (a_own, a_recv, *weights), name=name,
        )
        return kept, swap(sent, SPLIT)

    middle = HEAD_SIZE // 2
    exponent = jnp.arange(middle, dtype=jnp.float32) * (2.0 / HEAD_SIZE)
    positions = (ctx * rows + jnp.arange(rows, dtype=jnp.int32)).astype(jnp.float32)
    angles = positions[:, None] * (ROPE_BASE ** (-exponent))[None, :]
    cosine, sine = jnp.cos(angles), jnp.sin(angles)
    cosine = jnp.concatenate([cosine, cosine], axis=1)
    sine = jnp.concatenate([-sine, sine], axis=1)

    kept, came = project(gathered[0], "kv_project")
    n_blocks = kv_weight.shape[1] // HEAD_SIZE
    total = kept + came.astype(jnp.float32) + kv_bias.astype(jnp.float32)
    columns = []
    for b in range(n_blocks):
        v = total[:, b * HEAD_SIZE : (b + 1) * HEAD_SIZE]
        columns.append(jnp.where(rep * n_blocks + b < KEY_VALUE_HEADS, rotate(v, cosine, sine), v))
    kv_local = jnp.concatenate(columns, axis=1).astype(jnp.bfloat16)
    key_value_cache = gather_rep(kv_local, 1)
    leading = rep * local_heads // head_group
    used = [
        lax.dynamic_slice_in_dim(key_value_cache, (first + leading) * HEAD_SIZE, kv_heads * HEAD_SIZE, 1)
        for first in (0, KEY_VALUE_HEADS)
    ]
    cache = jnp.concatenate(used, axis=1)
    for bit in [SPLIT] + high_bits + [Y, CORE]:
        cache = jnp.concatenate([cache, swap(cache, bit)], axis=0)

    heads = q_cols // HEAD_SIZE
    inner = local_heads // kv_heads
    n_tokens = rows * n_ctx
    att_own, att_recv = [], []
    for i in range(n_q):
        kept, came = project(gathered[1 + i], f"q_project{i}")
        kv_head = i * heads // inner
        keys = cache[:, kv_head * HEAD_SIZE : (kv_head + 1) * HEAD_SIZE]
        values = cache[:, (kv_heads + kv_head) * HEAD_SIZE : (kv_heads + kv_head + 1) * HEAD_SIZE]
        (attended,) = call(
            functools.partial(attend_body, n_bits),
            (jax.ShapeDtypeStruct((rows, q_cols), jnp.bfloat16),),
            [SM] + [VM] * 7, 4 * heads * rows * n_tokens * HEAD_SIZE * 2, 2 * n_tokens * HEAD_SIZE * 2,
            (place, kept, came, q_bias[i * q_cols : (i + 1) * q_cols].reshape(1, q_cols), cosine, sine, keys, values),
            scratch=[
                pltpu.VMEM((heads * rows, HEAD_SIZE), jnp.bfloat16),
                pltpu.VMEM((heads * rows, HEAD_SIZE), jnp.float32),
                pltpu.VMEM((heads * rows, 1), jnp.float32),
                pltpu.VMEM((heads * rows, 1), jnp.float32),
            ],
            name=f"attend{i}",
        )
        att_own.append(attended)
        att_recv.append(swap(attended, SPLIT))

    size = rows // n_rep
    own, recv = [], []
    for s in range(n_out):
        weights = gathered[1 + n_q + s]
        n = out_cols * n_masks
        (partial,) = call(
            functools.partial(output_body, n_q),
            (jax.ShapeDtypeStruct((n_rep, 2 * size, n), jnp.bfloat16),),
            [SM] + [VM] * (2 * n_q + n_masks), 2 * 2 * rows * out_weight.shape[0] * n,
            2 * rows * out_weight.shape[0] * 2 + out_weight.shape[0] * n * 2,
            (place, *att_own, *att_recv, *weights), name=f"out_project{s}",
        )
        total = partial[0].astype(jnp.float32)
        for far in range(1, n_rep):
            total = total + swap_rep(partial[far], far).astype(jnp.float32)
        total = total.astype(jnp.bfloat16)
        own.append(total[:size])
        recv.append(swap(total[size:], SPLIT))
    (result,) = call(
        functools.partial(place_body, masks, n_out),
        (jax.ShapeDtypeStruct((size, width), jnp.bfloat16),),
        [SM] + [VM] * (2 * n_out), 0, 2 * size * width * 2, (place, *own, *recv), name="placed",
    )
    return result, key_value_cache


def solution(mesh):
    in_specs = (
        P("ctx", None),
        P(),
        P("ctx", "rep"),
        P("rep"),
        P("ctx", "rep"),
        P("rep"),
        P("rep", "ctx"),
    )
    out_specs = (P(("ctx", "rep"), None), P("ctx", None))
    return jax.shard_map(per_device, mesh=mesh, in_specs=in_specs, out_specs=out_specs, check_vma=False)
```

```python
import functools

import jax
import jax.numpy as jnp
from jax import lax
from jax.experimental import pallas as pl
from jax.experimental.pallas import tpu as pltpu
from jax.sharding import PartitionSpec as P

HEAD_SIZE = 128
QUERY_HEADS = 32
KEY_VALUE_HEADS = 4
ROPE_BASE = 1000000.0
CORE, Y, NEAR = 1, 2, 4
GROUP = (0, CORE, NEAR, NEAR | CORE)
VMEM_LIMIT = 48 * 1024 * 1024
LOG2E = 1.4426950408889634
VM = pl.BlockSpec(memory_space=pltpu.VMEM)
SM = pl.BlockSpec(memory_space=pltpu.SMEM)


def swap(x, mask):
    n = lax.axis_size("ctx")
    return lax.ppermute(x, "ctx", [(i, i ^ mask) for i in range(n)])


def swap_rep(x, mask):
    n = lax.axis_size("rep")
    return lax.ppermute(x, "rep", [(i, i ^ mask) for i in range(n)])


def after(x, *tokens):
    tokens = tuple(t for t in tokens if t is not None)
    if not tokens:
        return x
    return lax.optimization_barrier((x,) + tokens)[0]


def gather_rep(x, axis):
    rep = lax.axis_index("rep")
    bit = 1
    while bit < lax.axis_size("rep"):
        other = swap_rep(x, bit)
        high = (rep & bit) != 0
        x = jnp.concatenate([jnp.where(high, other, x), jnp.where(high, x, other)], axis=axis)
        bit *= 2
    return x


def call(body, out_shape, specs, flops, nbytes, args, scratch=(), name=None):
    outs = tuple(out_shape)
    return pl.pallas_call(
        body,
        out_shape=outs,
        in_specs=specs,
        out_specs=tuple(VM for _ in outs),
        scratch_shapes=list(scratch),
        compiler_params=pltpu.CompilerParams(vmem_limit_bytes=VMEM_LIMIT),
        cost_estimate=pl.CostEstimate(flops=flops, bytes_accessed=nbytes, transcendentals=0),
        name=name,
    )(*args)


def norm_body(masks, place, tokens, gain, own, core, far):
    ctx, rep = place[0], place[1]
    rows, width = tokens.shape
    kb = own.shape[1] // len(masks)
    step = 32
    share = far.shape[0]

    def normed(part, out_part, targets):
        t = tokens[part, :].astype(jnp.float32)
        scale = lax.rsqrt(jnp.sum(t * t, axis=-1, keepdims=True) * (1.0 / width) + 1e-06)
        for e, ref, first in targets:
            for j, m in enumerate(masks):
                block = pl.ds(pl.multiple_of((ctx ^ (m | e)) * kb, 128), kb)
                v = tokens[part, block].astype(jnp.float32) * scale * gain[:, block].astype(jnp.float32)
                ref[out_part, first + j * kb : first + (j + 1) * kb] = v.astype(jnp.bfloat16)

    def distant(i, carry):
        part = pl.ds(pl.multiple_of(rep * share + i * step, step), step)
        normed(part, pl.ds(i * step, step), ((NEAR, far, 0), (NEAR | CORE, far, own.shape[1])))
        return carry

    def local(i, carry):
        part = pl.ds(i * step, step)
        normed(part, part, ((0, own, 0), (CORE, core, 0)))
        return carry

    lax.fori_loop(0, share // step, distant, 0)
    lax.fori_loop(0, rows // step, local, 0)


def times(a, weights, columns):
    kb = weights[0].shape[0]
    total = None
    for j, w in enumerate(weights):
        part = jnp.dot(a[:, j * kb : (j + 1) * kb], w[:, columns], preferred_element_type=jnp.float32)
        total = part if total is None else total + part
    return total


def kv_body(a0, a1, a4, a5, *refs):
    weights, (kept, sent) = refs[:-2], refs[-2:]
    rows = a0.shape[0]
    for out, parts in ((kept, (a0, a4)), (sent, (a1, a5))):
        for i, a in enumerate(parts):
            out[i * rows : (i + 1) * rows, :] = times(a, weights, slice(None)).astype(out.dtype)


def query_body(place, a0, a1, a4, a5, *refs):
    weights, (kept, sent) = refs[:-2], refs[-2:]
    core = place[0] & 1
    rows, half = a0.shape[0], kept.shape[1]
    for i, a in enumerate((a0, a1, a4, a5)):
        mine = pl.ds(pl.multiple_of(core * half, 128), half)
        other = pl.ds(pl.multiple_of((1 - core) * half, 128), half)
        kept[i * rows : (i + 1) * rows, :] = times(a, weights, mine)
        turned = i ^ 1
        sent[turned * rows : (turned + 1) * rows, :] = times(a, weights, other).astype(jnp.bfloat16)


def halve_body(place, kept, came, mine, sent):
    near = (place[0] >> 2) & 1
    n = mine.shape[1]
    half = mine.shape[0] // 2
    here = pl.ds(pl.multiple_of(near * n, 128), n)
    there = pl.ds(pl.multiple_of((1 - near) * n, 128), n)
    mine[...] = kept[:, here] + came[:, here].astype(jnp.float32)
    for i in range(2):
        rows, turned = slice(i * half, (i + 1) * half), slice((1 - i) * half, (2 - i) * half)
        sent[turned, :] = (kept[rows, there] + came[rows, there].astype(jnp.float32)).astype(jnp.bfloat16)


def rotate(v, cosine, sine):
    half = HEAD_SIZE // 2
    turned = jnp.concatenate([v[:, half:], v[:, :half]], axis=1)
    return v * cosine + turned * sine


def attend_body(n_bits, place, mine, other, bias, cosine, sine, cache, out, q, acc, top):
    ctx = place[0]
    rows4, width = mine.shape
    rows = rows4 // 4
    pair = 2 * rows
    heads = width // HEAD_SIZE
    tile = heads * pair
    for h in range(heads):
        cols = slice(h * HEAD_SIZE, (h + 1) * HEAD_SIZE)
        v = mine[:, cols] + other[:, cols].astype(jnp.float32) + bias[:, cols].astype(jnp.float32)
        v = rotate(v, cosine[...], sine[...]).astype(jnp.bfloat16)
        for f in range(2):
            q[f * tile + h * pair : f * tile + (h + 1) * pair, :] = v[f * pair : (f + 1) * pair, :]
    factor = LOG2E * HEAD_SIZE ** (-0.5)
    ones = jnp.ones((pair, HEAD_SIZE), jnp.bfloat16)

    def place_of(k):
        return (k >> 2) | ((k & 2) << (n_bits - 3)) | ((k & 1) << (n_bits - 1))

    def load(k, first):
        spots = [pl.ds(pl.multiple_of(place_of(b) * rows, 128), rows) for b in (k, k ^ 1)]
        return jnp.concatenate([cache[s, first : first + HEAD_SIZE] for s in spots], axis=0)

    def scores(part, k):
        return lax.dot_general(
            q[part, :], load(k, 0), (((1,), (1,)), ((), ())), preferred_element_type=jnp.float32
        )

    def weighted(s, m, k):
        p = jnp.exp2((s - jnp.concatenate([m] * (pair // HEAD_SIZE), axis=1)) * factor).astype(jnp.bfloat16)
        return jnp.dot(p, jnp.concatenate([load(k, HEAD_SIZE), ones], axis=1), preferred_element_type=jnp.float32)

    def begin(f):
        part = slice(f * tile, (f + 1) * tile)
        s = scores(part, NEAR * f)
        r = lax.broadcasted_iota(jnp.int32, s.shape, 0) % pair
        c = lax.broadcasted_iota(jnp.int32, s.shape, 1)
        odd = ctx & 1
        row = ((r // rows) ^ odd) * rows + r % rows
        col = ((c // rows) ^ odd) * rows + c % rows
        s = jnp.where(col <= row, s, -1e30)
        m = jnp.broadcast_to(jnp.max(s, axis=-1, keepdims=True), (tile, HEAD_SIZE))
        top[part, :] = m
        acc[part, :] = weighted(s, m, NEAR * f)

    def step(start, k):
        part = pl.ds(start, tile)
        s = scores(part, k)
        old = top[part, :]
        m = jnp.maximum(old, jnp.max(s, axis=-1, keepdims=True))
        top[part, :] = m
        shrink = jnp.exp2((old - m) * factor)
        acc[part, :] = acc[part, :] * jnp.concatenate([shrink, shrink], axis=1) + weighted(s, m, k)

    begin(0)
    begin(1)
    here, there = ctx >> 1, (ctx ^ NEAR) >> 1
    common = jnp.minimum(here, there)

    def both(b, carry):
        k = ctx ^ (2 * b)
        step(0, k)
        step(tile, k)
        return carry

    def single(b, carry):
        step(pl.multiple_of(jnp.where(here > there, 0, tile), 128), ctx ^ (2 * b))
        return carry

    lax.fori_loop(0, common, both, 0)
    lax.fori_loop(common, jnp.maximum(here, there), single, 0)
    for f in range(2):
        for h in range(heads):
            a = acc[f * tile + h * pair : f * tile + (h + 1) * pair, :]
            part = (a[:, :HEAD_SIZE] / a[:, HEAD_SIZE:]).astype(jnp.bfloat16)
            out[f * pair : (f + 1) * pair, h * HEAD_SIZE : (h + 1) * HEAD_SIZE] = part


def collect_body(n_parts, heads_each, place, *refs):
    pieces, out = refs[:-1], refs[-1]
    ctx, rep = place[0], place[1]
    rows = pieces[0].shape[0] // 4
    wide = pieces[0].shape[1]
    members = out.shape[0]
    size = rows // members
    for d, distance in enumerate(GROUP):
        owner = ctx ^ distance
        group = ((owner >> 2) & 1) * 2 + (owner & 1)
        for i in range(n_parts):
            piece = pieces[d * n_parts + i]
            column = pl.ds(pl.multiple_of(group * (n_parts * wide) + i * wide, 128), wide)
            for far in range(members):
                for e in range(4):
                    part = pl.ds(pl.multiple_of((e ^ d) * rows + (rep ^ far) * size, size), size)
                    out[far, e * size : (e + 1) * size, column] = piece[part, :]


def output_body(att, *refs):
    weights, out = refs[:-1], refs[-1]
    n = weights[0].shape[1]
    for far in range(att.shape[0]):
        for j, w in enumerate(weights):
            out[far, :, j * n : (j + 1) * n] = jnp.dot(
                att[far], w[...], preferred_element_type=jnp.float32
            ).astype(jnp.bfloat16)


def place_body(masks, n_sub, place, *refs):
    sums, fars, cores, out = refs[:n_sub], refs[n_sub : 2 * n_sub], refs[2 * n_sub : -1], refs[-1]
    ctx = place[0]
    size = out.shape[0]
    sub = sums[0].shape[1] // len(masks)
    for s in range(n_sub):
        sources = ((0, sums[s], 0), (NEAR, fars[s], 0), (CORE, cores[s], 0), (NEAR | CORE, cores[s], size))
        for e, ref, first in sources:
            for j, m in enumerate(masks):
                start = (ctx ^ (m | e)) * (sub * n_sub) + s * sub
                out[:, pl.ds(pl.multiple_of(start, 128), sub)] = ref[first : first + size, j * sub : (j + 1) * sub]


class Stream:
    def __init__(self, depth):
        self.depth, self.done = depth, []

    def swap(self, x, mask):
        if len(self.done) >= self.depth:
            x = after(x, self.done[-self.depth])
        got = swap(x, mask)
        self.done.append(got)
        return got


def per_device(tokens, norm_gain, q_weight, q_bias, kv_weight, kv_bias, out_weight):
    rows, width = tokens.shape
    n_ctx, n_rep = lax.axis_size("ctx"), lax.axis_size("rep")
    n_bits = n_ctx.bit_length() - 1
    ctx, rep = lax.axis_index("ctx"), lax.axis_index("rep")
    place = jnp.stack([ctx, rep]).astype(jnp.int32)
    head_group = QUERY_HEADS // KEY_VALUE_HEADS
    local_heads = q_weight.shape[1] // HEAD_SIZE
    own_heads = local_heads // 4
    high_bits = [1 << b for b in range(3, n_bits)]
    masks = [0]
    for bit in high_bits + [Y]:
        masks = masks + [m | bit for m in masks]
    masks = sorted(masks)
    n_masks = len(masks)

    n_q = min(4, own_heads)
    heads = own_heads // n_q
    n = heads * HEAD_SIZE
    groups = q_weight.reshape(q_weight.shape[0], 2, 2, n_q, n)
    groups = jnp.swapaxes(groups, 1, 2)
    bias = q_bias.reshape(4, n_q, n)
    n_out = max(1, min(4, out_weight.shape[1] // 128))
    out_cols = out_weight.shape[1] // n_out
    pieces = {"kv": kv_weight}
    for i in range(n_q):
        pieces[f"q{i}"] = groups[:, :, :, i].reshape(q_weight.shape[0], 4 * n)
    for i in range(n_out):
        pieces[f"o{i}"] = out_weight[:, i * out_cols : (i + 1) * out_cols]
    blocks = {name: {0: piece} for name, piece in pieces.items()}
    z_stream, y_stream = Stream(2), Stream(2)

    def high(name):
        if name in blocks:
            for bit in high_bits:
                for m in list(blocks[name]):
                    blocks[name][m | bit] = z_stream.swap(blocks[name][m], bit)

    def first(name):
        if name in blocks:
            blocks[name][Y] = y_stream.swap(blocks[name][0], Y)

    def rest(name):
        if name in blocks:
            for m in sorted(blocks[name]):
                if m and not m & Y:
                    blocks[name][m | Y] = y_stream.swap(blocks[name][m], Y)

    def weights(name):
        return [blocks[name][m] for m in masks]

    high("kv")
    first("kv")
    high("q0")
    first("q0")
    rest("kv")

    kw = width // 4
    a_own, a_core, a_far = call(
        functools.partial(norm_body, masks),
        (
            jax.ShapeDtypeStruct((rows, kw), jnp.bfloat16),
            jax.ShapeDtypeStruct((rows, kw), jnp.bfloat16),
            jax.ShapeDtypeStruct((rows // n_rep, 2 * kw), jnp.bfloat16),
        ),
        [SM, VM, VM], 0, 3 * rows * width * 2, (place, tokens, norm_gain.reshape(1, width)), name="normed",
    )
    a_1 = swap(a_core, CORE)
    a_via = gather_rep(swap(a_far[:, kw:], NEAR), 0)
    a_4 = gather_rep(swap(a_far[:, :kw], NEAR), 0)
    a_5 = swap(a_via, CORE)
    shares = (a_own, a_1, a_4, a_5)

    high("q1")
    first("q1")
    rest("q0")
    high("q2")
    first("q2")
    rest("q1")

    middle = HEAD_SIZE // 2
    exponent = jnp.arange(middle, dtype=jnp.float32) * (2.0 / HEAD_SIZE)
    starts = jnp.stack([(ctx ^ e) * rows for e in GROUP])
    positions = (starts[:, None] + jnp.arange(rows, dtype=jnp.int32)[None, :]).reshape(-1).astype(jnp.float32)
    angles = positions[:, None] * (ROPE_BASE ** (-exponent))[None, :]
    cosine, sine = jnp.cos(angles), jnp.sin(angles)
    cosine = jnp.concatenate([cosine, cosine], axis=1)
    sine = jnp.concatenate([-sine, sine], axis=1)

    kv_cols = kv_weight.shape[1]
    kept, sent = call(
        kv_body,
        (
            jax.ShapeDtypeStruct((2 * rows, kv_cols), jnp.float32),
            jax.ShapeDtypeStruct((2 * rows, kv_cols), jnp.bfloat16),
        ),
        [VM] * (4 + n_masks), 8 * rows * kw * kv_cols, 2 * kw * (4 * rows + kv_cols),
        (*shares, *weights("kv")), name="kv_project",
    )
    total = kept + swap(sent, CORE).astype(jnp.float32)
    total = total[:rows] + swap(total[rows:].astype(jnp.bfloat16), NEAR).astype(jnp.float32)
    total = total + kv_bias.astype(jnp.float32)
    n_blocks = kv_cols // HEAD_SIZE
    columns = []
    for b in range(n_blocks):
        v = total[:, b * HEAD_SIZE : (b + 1) * HEAD_SIZE]
        columns.append(jnp.where(rep * n_blocks + b < KEY_VALUE_HEADS, rotate(v, cosine[:rows], sine[:rows]), v))
    kv_local = jnp.concatenate(columns, axis=1).astype(jnp.bfloat16)
    key_value_cache = gather_rep(kv_local, 1)

    def used(near):
        head = (rep * local_heads + near * (local_heads // 2)) // head_group
        parts = [
            lax.dynamic_slice_in_dim(key_value_cache, (offset + head) * HEAD_SIZE, HEAD_SIZE, 1)
            for offset in (0, KEY_VALUE_HEADS)
        ]
        return jnp.concatenate(parts, axis=1)

    near = (ctx >> 2) & 1
    cache = jnp.concatenate([used(near), swap(used(1 - near), NEAR)], axis=0)
    for bit in high_bits:
        cache = jnp.concatenate([cache, z_stream.swap(cache, bit)], axis=0)
    high("q3")
    first("q3")
    rest("q2")
    first("o0")
    cache = jnp.concatenate([cache, y_stream.swap(cache, Y)], axis=0)
    cache = jnp.concatenate([cache, swap(cache, CORE)], axis=0)
    rest("q3")
    for i in range(n_out):
        high(f"o{i}")
        first(f"o{i + 1}")
        rest(f"o{i}")

    n_tokens = rows * n_ctx
    own_bias = lax.dynamic_index_in_dim(bias, near * 2 + (ctx & 1), 0, keepdims=False)
    att = {d: [] for d in GROUP}
    for i in range(n_q):
        kept, sent = call(
            query_body,
            (
                jax.ShapeDtypeStruct((4 * rows, 2 * n), jnp.float32),
                jax.ShapeDtypeStruct((4 * rows, 2 * n), jnp.bfloat16),
            ),
            [SM] + [VM] * (4 + n_masks), 8 * rows * kw * 4 * n, 2 * kw * (4 * rows + 4 * n),
            (place, *shares, *weights(f"q{i}")), name=f"q_project{i}",
        )
        mine, sent = call(
            halve_body,
            (jax.ShapeDtypeStruct((4 * rows, n), jnp.float32), jax.ShapeDtypeStruct((4 * rows, n), jnp.bfloat16)),
            [SM, VM, VM], 0, 4 * rows * n * 18, (place, kept, swap(sent, CORE)), name=f"q_halve{i}",
        )
        (attended,) = call(
            functools.partial(attend_body, n_bits),
            (jax.ShapeDtypeStruct((4 * rows, n), jnp.bfloat16),),
            [SM] + [VM] * 6, 4 * heads * 4 * rows * n_tokens * HEAD_SIZE * 2, 2 * n_tokens * HEAD_SIZE * 2,
            (place, mine, swap(sent, NEAR), own_bias[i : i + 1], cosine, sine, cache),
            scratch=[
                pltpu.VMEM((4 * heads * rows, HEAD_SIZE), jnp.bfloat16),
                pltpu.VMEM((4 * heads * rows, 2 * HEAD_SIZE), jnp.float32),
                pltpu.VMEM((4 * heads * rows, HEAD_SIZE), jnp.float32),
            ],
            name=f"attend{i}",
        )
        far = swap(attended, NEAR)
        att[0].append(attended)
        att[NEAR].append(far)
        att[CORE].append(swap(attended, CORE))
        att[NEAR | CORE].append(swap(far, CORE))
    size = rows // n_rep
    (collected,) = call(
        functools.partial(collect_body, n_q, heads),
        (jax.ShapeDtypeStruct((n_rep, 4 * size, local_heads * HEAD_SIZE), jnp.bfloat16),),
        [SM] + [VM] * (4 * n_q), 0, 16 * rows * local_heads * HEAD_SIZE,
        (place, *[a for d in GROUP for a in att[d]]), name="collected",
    )

    sums, fars, cores = [], [], []
    for s in range(n_out):
        cols = out_cols * n_masks
        (partial,) = call(
            output_body,
            (jax.ShapeDtypeStruct((n_rep, 4 * size, cols), jnp.bfloat16),),
            [VM] * (1 + n_masks), 8 * rows * out_weight.shape[0] * cols,
            2 * out_weight.shape[0] * (4 * rows + cols) + 8 * rows * cols,
            (collected, *weights(f"o{s}")), name=f"out_project{s}",
        )
        total = partial[0].astype(jnp.float32)
        for far in range(1, n_rep):
            total = total + swap_rep(partial[far], far).astype(jnp.float32)
        total = total.astype(jnp.bfloat16)
        came = swap(total[2 * size :], NEAR)
        sums.append(total)
        fars.append(came)
        cores.append(swap(jnp.concatenate([total[size : 2 * size], came[size:]], axis=0), CORE))
    (result,) = call(
        functools.partial(place_body, masks, n_out),
        (jax.ShapeDtypeStruct((size, width), jnp.bfloat16),),
        [SM] + [VM] * (3 * n_out), 0, 2 * size * width * 2, (place, *sums, *fars, *cores), name="placed",
    )
    return result, key_value_cache


def solution(mesh):
    in_specs = (
        P("ctx", None),
        P(),
        P("ctx", "rep"),
        P("rep"),
        P("ctx", "rep"),
        P("rep"),
        P("rep", "ctx"),
    )
    out_specs = (P(("ctx", "rep"), None), P("ctx", None))
    return jax.shard_map(per_device, mesh=mesh, in_specs=in_specs, out_specs=out_specs, check_vma=False)
```

```python
import functools

import jax
import jax.numpy as jnp
from jax import lax
from jax.experimental import pallas as pl
from jax.experimental.pallas import tpu as pltpu
from jax.sharding import PartitionSpec as P

HEAD_SIZE = 128
QUERY_HEADS = 32
KEY_VALUE_HEADS = 4
ROPE_BASE = 1000000.0
CORE, Y, NEAR = 1, 2, 4
GROUP = (0, CORE, NEAR, NEAR | CORE)
VMEM_LIMIT = 48 * 1024 * 1024
COST = 3
LOG2E = 1.4426950408889634
VM = pl.BlockSpec(memory_space=pltpu.VMEM)
SM = pl.BlockSpec(memory_space=pltpu.SMEM)


def swap(x, mask):
    n = lax.axis_size("ctx")
    return lax.ppermute(x, "ctx", [(i, i ^ mask) for i in range(n)])


def swap_rep(x, mask):
    n = lax.axis_size("rep")
    return lax.ppermute(x, "rep", [(i, i ^ mask) for i in range(n)])


class Cell:
    def __init__(self, value):
        self.v = value


def after(x, *cells):
    cells = [c for c in cells if c is not None]
    if not cells:
        return x
    results = lax.optimization_barrier((x, *[c.v for c in cells]))
    for c, v in zip(cells, results[1:]):
        c.v = v
    return results[0]


def gather_rep(x, axis):
    rep = lax.axis_index("rep")
    bit = 1
    while bit < lax.axis_size("rep"):
        other = swap_rep(x, bit)
        high = (rep & bit) != 0
        x = jnp.concatenate([jnp.where(high, other, x), jnp.where(high, x, other)], axis=axis)
        bit *= 2
    return x


def call(body, out_shape, specs, flops, nbytes, args, scratch=(), name=None):
    outs = tuple(out_shape)
    return pl.pallas_call(
        body,
        out_shape=outs,
        in_specs=specs,
        out_specs=tuple(VM for _ in outs),
        scratch_shapes=list(scratch),
        compiler_params=pltpu.CompilerParams(vmem_limit_bytes=VMEM_LIMIT),
        cost_estimate=pl.CostEstimate(flops=int(flops * COST), bytes_accessed=int(nbytes * COST), transcendentals=0),
        name=name,
    )(*args)


def norm_body(masks, place, tokens, gain, own, core, far):
    ctx, rep = place[0], place[1]
    rows, width = tokens.shape
    kb = own.shape[1] // len(masks)
    step = 32
    share = far.shape[0]

    def normed(part, out_part, targets):
        t = tokens[part, :].astype(jnp.float32)
        scale = lax.rsqrt(jnp.sum(t * t, axis=-1, keepdims=True) * (1.0 / width) + 1e-06)
        for e, ref, first in targets:
            for j, m in enumerate(masks):
                block = pl.ds(pl.multiple_of((ctx ^ (m | e)) * kb, 128), kb)
                v = tokens[part, block].astype(jnp.float32) * scale * gain[:, block].astype(jnp.float32)
                ref[out_part, first + j * kb : first + (j + 1) * kb] = v.astype(jnp.bfloat16)

    def distant(i, carry):
        part = pl.ds(pl.multiple_of(rep * share + i * step, step), step)
        normed(part, pl.ds(i * step, step), ((NEAR, far, 0), (NEAR | CORE, far, own.shape[1])))
        return carry

    def local(i, carry):
        part = pl.ds(i * step, step)
        normed(part, part, ((0, own, 0), (CORE, core, 0)))
        return carry

    lax.fori_loop(0, share // step, distant, 0)
    lax.fori_loop(0, rows // step, local, 0)


def times(a, weights, columns):
    kb = weights[0].shape[0]
    total = None
    for j, w in enumerate(weights):
        part = jnp.dot(a[:, j * kb : (j + 1) * kb], w[:, columns], preferred_element_type=jnp.float32)
        total = part if total is None else total + part
    return total


def kv_body(n_share, place, own, core, *refs):
    near, cross = refs[:n_share], refs[n_share : 2 * n_share]
    weights, (kept, sent, joined) = refs[2 * n_share : -3], refs[-3:]
    rep = place[1]
    rows = own.shape[0]
    share = rows // n_share
    joined[0:rows, :] = own[...]
    joined[rows : 2 * rows, :] = core[...]
    for i, parts in ((2, near), (3, cross)):
        for far, part in enumerate(parts):
            start = pl.multiple_of(i * rows + (rep ^ far) * share, share)
            joined[pl.ds(start, share), :] = part[...]
    for i in range(4):
        out = sent if i & 1 else kept
        half = slice((i >> 1) * rows, ((i >> 1) + 1) * rows)
        out[half, :] = times(joined[i * rows : (i + 1) * rows, :], weights, slice(None)).astype(out.dtype)


def query_body(place, joined, *refs):
    weights, (kept, sent) = refs[:-2], refs[-2:]
    core = place[0] & 1
    rows, half = joined.shape[0] // 4, kept.shape[1]
    mine = pl.ds(pl.multiple_of(core * half, 128), half)
    other = pl.ds(pl.multiple_of((1 - core) * half, 128), half)
    kept[...] = times(joined, weights, mine)
    product = times(joined, weights, other).astype(jnp.bfloat16)
    for i in range(4):
        turned = i ^ 1
        sent[turned * rows : (turned + 1) * rows, :] = product[i * rows : (i + 1) * rows, :]


def halve_body(place, kept, came, mine, sent):
    near = (place[0] >> 2) & 1
    n = mine.shape[1]
    half = mine.shape[0] // 2
    here = pl.ds(pl.multiple_of(near * n, 128), n)
    there = pl.ds(pl.multiple_of((1 - near) * n, 128), n)
    mine[...] = kept[:, here] + came[:, here].astype(jnp.float32)
    for i in range(2):
        rows, turned = slice(i * half, (i + 1) * half), slice((1 - i) * half, (2 - i) * half)
        sent[turned, :] = (kept[rows, there] + came[rows, there].astype(jnp.float32)).astype(jnp.bfloat16)


def rotate(v, cosine, sine):
    half = HEAD_SIZE // 2
    turned = jnp.concatenate([v[:, half:], v[:, :half]], axis=1)
    return v * cosine + turned * sine


def attend_body(n_bits, place, mine, other, bias, cosine, sine, cache, out, q, acc, top):
    ctx = place[0]
    rows4, width = mine.shape
    rows = rows4 // 4
    pair = 2 * rows
    heads = width // HEAD_SIZE
    tile = heads * pair
    for h in range(heads):
        cols = slice(h * HEAD_SIZE, (h + 1) * HEAD_SIZE)
        v = mine[:, cols] + other[:, cols].astype(jnp.float32) + bias[:, cols].astype(jnp.float32)
        v = rotate(v, cosine[...], sine[...]).astype(jnp.bfloat16)
        for f in range(2):
            q[f * tile + h * pair : f * tile + (h + 1) * pair, :] = v[f * pair : (f + 1) * pair, :]
    factor = LOG2E * HEAD_SIZE ** (-0.5)
    ones = jnp.ones((pair, HEAD_SIZE), jnp.bfloat16)

    def place_of(k):
        return (k >> 2) | ((k & 2) << (n_bits - 3)) | ((k & 1) << (n_bits - 1))

    def load(k, first):
        spots = [pl.ds(pl.multiple_of(place_of(b) * rows, 128), rows) for b in (k, k ^ 1)]
        return jnp.concatenate([cache[s, first : first + HEAD_SIZE] for s in spots], axis=0)

    def scores(part, k):
        return lax.dot_general(
            q[part, :], load(k, 0), (((1,), (1,)), ((), ())), preferred_element_type=jnp.float32
        )

    def weighted(s, m, k):
        p = jnp.exp2((s - jnp.concatenate([m] * (pair // HEAD_SIZE), axis=1)) * factor).astype(jnp.bfloat16)
        return jnp.dot(p, jnp.concatenate([load(k, HEAD_SIZE), ones], axis=1), preferred_element_type=jnp.float32)

    def begin(f):
        part = slice(f * tile, (f + 1) * tile)
        s = scores(part, NEAR * f)
        r = lax.broadcasted_iota(jnp.int32, s.shape, 0) % pair
        c = lax.broadcasted_iota(jnp.int32, s.shape, 1)
        odd = ctx & 1
        row = ((r // rows) ^ odd) * rows + r % rows
        col = ((c // rows) ^ odd) * rows + c % rows
        s = jnp.where(col <= row, s, -1e30)
        m = jnp.broadcast_to(jnp.max(s, axis=-1, keepdims=True), (tile, HEAD_SIZE))
        top[part, :] = m
        acc[part, :] = weighted(s, m, NEAR * f)

    def step(start, k):
        part = pl.ds(start, tile)
        s = scores(part, k)
        old = top[part, :]
        m = jnp.maximum(old, jnp.max(s, axis=-1, keepdims=True))
        top[part, :] = m
        shrink = jnp.exp2((old - m) * factor)
        acc[part, :] = acc[part, :] * jnp.concatenate([shrink, shrink], axis=1) + weighted(s, m, k)

    begin(0)
    begin(1)
    here, there = ctx >> 1, (ctx ^ NEAR) >> 1
    common = jnp.minimum(here, there)

    def both(b, carry):
        k = ctx ^ (2 * b)
        step(0, k)
        step(tile, k)
        return carry

    def single(b, carry):
        step(pl.multiple_of(jnp.where(here > there, 0, tile), 128), ctx ^ (2 * b))
        return carry

    lax.fori_loop(0, common, both, 0)
    lax.fori_loop(common, jnp.maximum(here, there), single, 0)
    for f in range(2):
        for h in range(heads):
            a = acc[f * tile + h * pair : f * tile + (h + 1) * pair, :]
            part = (a[:, :HEAD_SIZE] / a[:, HEAD_SIZE:]).astype(jnp.bfloat16)
            out[f * pair : (f + 1) * pair, h * HEAD_SIZE : (h + 1) * HEAD_SIZE] = part


def collect_body(n_parts, heads_each, place, *refs):
    pieces, out = refs[:-1], refs[-1]
    ctx, rep = place[0], place[1]
    rows = pieces[0].shape[0] // 4
    wide = pieces[0].shape[1]
    members = out.shape[0]
    size = rows // members
    for d, distance in enumerate(GROUP):
        owner = ctx ^ distance
        group = ((owner >> 2) & 1) * 2 + (owner & 1)
        for i in range(n_parts):
            piece = pieces[d * n_parts + i]
            column = pl.ds(pl.multiple_of(group * (n_parts * wide) + i * wide, 128), wide)
            for far in range(members):
                for e in range(4):
                    part = pl.ds(pl.multiple_of((e ^ d) * rows + (rep ^ far) * size, size), size)
                    out[far, e * size : (e + 1) * size, column] = piece[part, :]


def output_body(att, *refs):
    weights, out = refs[:-1], refs[-1]
    n = weights[0].shape[1]
    join = 2 if n < 256 and len(weights) % 2 == 0 else 1
    for far in range(att.shape[0]):
        for j in range(0, len(weights), join):
            w = jnp.concatenate([weights[j + i][...] for i in range(join)], axis=1)
            product = jnp.dot(att[far], w, preferred_element_type=jnp.float32)
            out[far, :, j * n : (j + join) * n] = product.astype(jnp.bfloat16)


def place_body(masks, n_sub, place, *refs):
    sums, fars, cores, out = refs[:n_sub], refs[n_sub : 2 * n_sub], refs[2 * n_sub : -1], refs[-1]
    ctx = place[0]
    size = out.shape[0]
    sub = sums[0].shape[1] // len(masks)
    for s in range(n_sub):
        sources = ((0, sums[s], 0), (NEAR, fars[s], 0), (CORE, cores[s], 0), (NEAR | CORE, cores[s], size))
        for e, ref, first in sources:
            for j, m in enumerate(masks):
                start = (ctx ^ (m | e)) * (sub * n_sub) + s * sub
                out[:, pl.ds(pl.multiple_of(start, 128), sub)] = ref[first : first + size, j * sub : (j + 1) * sub]


class Stream:
    def __init__(self):
        self.last = None

    def swap(self, x, mask, *cells):
        cells = [c for c in cells if c is not self.last]
        self.last = Cell(swap(after(x, self.last, *cells), mask))
        return self.last


def per_device(tokens, norm_gain, q_weight, q_bias, kv_weight, kv_bias, out_weight):
    rows, width = tokens.shape
    n_ctx, n_rep = lax.axis_size("ctx"), lax.axis_size("rep")
    n_bits = n_ctx.bit_length() - 1
    ctx, rep = lax.axis_index("ctx"), lax.axis_index("rep")
    place = jnp.stack([ctx, rep]).astype(jnp.int32)
    head_group = QUERY_HEADS // KEY_VALUE_HEADS
    local_heads = q_weight.shape[1] // HEAD_SIZE
    own_heads = local_heads // 4
    high_bits = [1 << b for b in range(3, n_bits)]
    masks = [0]
    for bit in high_bits + [Y]:
        masks = masks + [m | bit for m in masks]
    masks = sorted(masks)
    n_masks = len(masks)

    n_q = min(4, own_heads)
    heads = own_heads // n_q
    n = heads * HEAD_SIZE
    bias = q_bias.reshape(4, n_q, n)
    n_out = max(1, min(4, out_weight.shape[1] // 128))
    out_cols = out_weight.shape[1] // n_out
    pieces = {"kv": kv_weight}
    for i in range(n_q):
        columns = [((z * 2 + c) * n_q + i) * n for c in range(2) for z in range(2)]
        pieces[f"q{i}"] = jnp.concatenate([q_weight[:, first : first + n] for first in columns], axis=1)
    for i in range(n_out):
        pieces[f"o{i}"] = out_weight[:, i * out_cols : (i + 1) * out_cols]
    blocks = {name: {0: Cell(piece)} for name, piece in pieces.items()}
    z_stream, own_stream, y_stream = Stream(), Stream(), Stream()

    def step(name):
        if name in blocks:
            before = (z_stream.last, own_stream.last)
            for bit in high_bits:
                for m in sorted(blocks[name]):
                    blocks[name][m | bit] = z_stream.swap(blocks[name][m].v, bit, *before)
            blocks[name][Y] = own_stream.swap(blocks[name][0].v, Y, *before)

    def rest(name):
        if name in blocks:
            for m in sorted(blocks[name]):
                if m and not m & Y:
                    blocks[name][m | Y] = y_stream.swap(blocks[name][m].v, Y)

    def weights(name):
        return [blocks[name][m].v for m in masks]

    def z_of(name):
        return blocks[name][max(m for m in masks if not m & Y)] if name in blocks and high_bits else None

    def y_of(name):
        return blocks[name][Y] if name in blocks else None

    step("kv")
    step("q0")
    rest("kv")
    step("q1")
    rest("q0")
    step("q2")
    rest("q1")

    kw = width // 4
    share = rows // n_rep
    a_own, a_core, a_far = call(
        functools.partial(norm_body, masks),
        (
            jax.ShapeDtypeStruct((rows, kw), jnp.bfloat16),
            jax.ShapeDtypeStruct((rows, kw), jnp.bfloat16),
            jax.ShapeDtypeStruct((share, 2 * kw), jnp.bfloat16),
        ),
        [SM, VM, VM], 0, 3 * rows * width * 2, (place, tokens, norm_gain.reshape(1, width)), name="normed",
    )
    a_core = swap(a_core, CORE)
    cross = swap(a_far[:, kw:], NEAR)
    near_share = swap(a_far[:, :kw], NEAR)
    cross = after(cross, z_of("kv"), y_of("kv"))
    cross = [cross] + [swap_rep(cross, far) for far in range(1, n_rep)]
    near_share = [near_share] + [swap_rep(near_share, far) for far in range(1, n_rep)]
    cross = [swap(x, CORE) for x in cross]
    shares = (a_own, a_core, *near_share, *cross)
    middle = HEAD_SIZE // 2
    exponent = jnp.arange(middle, dtype=jnp.float32) * (2.0 / HEAD_SIZE)
    starts = jnp.stack([(ctx ^ e) * rows for e in GROUP])
    positions = (starts[:, None] + jnp.arange(rows, dtype=jnp.int32)[None, :]).reshape(-1).astype(jnp.float32)
    angles = positions[:, None] * (ROPE_BASE ** (-exponent))[None, :]
    cosine, sine = jnp.cos(angles), jnp.sin(angles)
    cosine = jnp.concatenate([cosine, cosine], axis=1)
    sine = jnp.concatenate([-sine, sine], axis=1)

    kv_cols = kv_weight.shape[1]
    kept, sent, joined = call(
        functools.partial(kv_body, n_rep),
        (
            jax.ShapeDtypeStruct((2 * rows, kv_cols), jnp.float32),
            jax.ShapeDtypeStruct((2 * rows, kv_cols), jnp.bfloat16),
            jax.ShapeDtypeStruct((4 * rows, kw), jnp.bfloat16),
        ),
        [SM] + [VM] * (2 + 2 * n_rep + n_masks), 8 * rows * kw * kv_cols, 2 * kw * (8 * rows + kv_cols),
        (place, *shares, *weights("kv")), name="kv_project",
    )
    total = kept + swap(sent, CORE).astype(jnp.float32)
    total = total[:rows] + swap(total[rows:].astype(jnp.bfloat16), NEAR).astype(jnp.float32)
    total = total + kv_bias.astype(jnp.float32)
    n_blocks = kv_cols // HEAD_SIZE
    columns = []
    for b in range(n_blocks):
        v = total[:, b * HEAD_SIZE : (b + 1) * HEAD_SIZE]
        columns.append(jnp.where(rep * n_blocks + b < KEY_VALUE_HEADS, rotate(v, cosine[:rows], sine[:rows]), v))
    kv_local = jnp.concatenate(columns, axis=1).astype(jnp.bfloat16)
    key_value_cache = gather_rep(kv_local, 1)

    def used(near):
        head = (rep * local_heads + near * (local_heads // 2)) // head_group
        parts = [
            lax.dynamic_slice_in_dim(key_value_cache, (offset + head) * HEAD_SIZE, HEAD_SIZE, 1)
            for offset in (0, KEY_VALUE_HEADS)
        ]
        return jnp.concatenate(parts, axis=1)

    near = (ctx >> 2) & 1
    cache = jnp.concatenate([used(near), swap(used(1 - near), NEAR)], axis=0)
    rest("q2")
    came = []
    for bit in high_bits:
        came.append((cache, z_stream.swap(cache, bit)))
        cache = jnp.concatenate([cache, came[-1][1].v], axis=0)
    step("q3")
    cache = jnp.concatenate([came[-1][0], came[-1][1].v], axis=0)
    other = y_stream.swap(cache, Y)
    rest("q3")
    for i in range(n_out):
        step(f"o{i}")
        rest(f"o{i}")
    cache = jnp.concatenate([cache, other.v], axis=0)
    cache = jnp.concatenate([cache, swap(cache, CORE)], axis=0)

    n_tokens = rows * n_ctx
    own_bias = lax.dynamic_index_in_dim(bias, near * 2 + (ctx & 1), 0, keepdims=False)
    att = {d: [] for d in GROUP}
    for i in range(n_q):
        kept, sent = call(
            query_body,
            (
                jax.ShapeDtypeStruct((4 * rows, 2 * n), jnp.float32),
                jax.ShapeDtypeStruct((4 * rows, 2 * n), jnp.bfloat16),
            ),
            [SM] + [VM] * (1 + n_masks), 8 * rows * kw * 4 * n, 2 * kw * (4 * rows + 4 * n),
            (place, joined, *weights(f"q{i}")), name=f"q_project{i}",
        )
        mine, sent = call(
            halve_body,
            (jax.ShapeDtypeStruct((4 * rows, n), jnp.float32), jax.ShapeDtypeStruct((4 * rows, n), jnp.bfloat16)),
            [SM, VM, VM], 0, 4 * rows * n * 18, (place, kept, swap(sent, CORE)), name=f"q_halve{i}",
        )
        (attended,) = call(
            functools.partial(attend_body, n_bits),
            (jax.ShapeDtypeStruct((4 * rows, n), jnp.bfloat16),),
            [SM] + [VM] * 6, 4 * heads * 4 * rows * n_tokens * HEAD_SIZE * 2, 2 * n_tokens * HEAD_SIZE * 2,
            (place, mine, swap(sent, NEAR), own_bias[i : i + 1], cosine, sine, cache),
            scratch=[
                pltpu.VMEM((4 * heads * rows, HEAD_SIZE), jnp.bfloat16),
                pltpu.VMEM((4 * heads * rows, 2 * HEAD_SIZE), jnp.float32),
                pltpu.VMEM((4 * heads * rows, HEAD_SIZE), jnp.float32),
            ],
            name=f"attend{i}",
        )
        far = swap(attended, NEAR)
        att[0].append(attended)
        att[NEAR].append(far)
        att[CORE].append(swap(attended, CORE))
        att[NEAR | CORE].append(swap(far, CORE))
    size = rows // n_rep
    (collected,) = call(
        functools.partial(collect_body, n_q, heads),
        (jax.ShapeDtypeStruct((n_rep, 4 * size, local_heads * HEAD_SIZE), jnp.bfloat16),),
        [SM] + [VM] * (4 * n_q), 0, 16 * rows * local_heads * HEAD_SIZE,
        (place, *[a for d in GROUP for a in att[d]]), name="collected",
    )

    sums, fars, cores = [], [], []
    for s in range(n_out):
        cols = out_cols * n_masks
        (partial,) = call(
            output_body,
            (jax.ShapeDtypeStruct((n_rep, 4 * size, cols), jnp.bfloat16),),
            [VM] * (1 + n_masks), 8 * rows * out_weight.shape[0] * cols,
            2 * out_weight.shape[0] * (4 * rows + cols) + 8 * rows * cols,
            (collected, *weights(f"o{s}")), name=f"out_project{s}",
        )
        total = partial[0].astype(jnp.float32)
        for far in range(1, n_rep):
            total = total + swap_rep(partial[far], far).astype(jnp.float32)
        total = total.astype(jnp.bfloat16)
        came = swap(total[2 * size :], NEAR)
        sums.append(total)
        fars.append(came)
        cores.append(swap(jnp.concatenate([total[size : 2 * size], came[size:]], axis=0), CORE))
    (result,) = call(
        functools.partial(place_body, masks, n_out),
        (jax.ShapeDtypeStruct((size, width), jnp.bfloat16),),
        [SM] + [VM] * (3 * n_out), 0, 2 * size * width * 2, (place, *sums, *fars, *cores), name="placed",
    )
    return result, key_value_cache


def solution(mesh):
    in_specs = (
        P("ctx", None),
        P(),
        P("ctx", "rep"),
        P("rep"),
        P("ctx", "rep"),
        P("rep"),
        P("rep", "ctx"),
    )
    out_specs = (P(("ctx", "rep"), None), P("ctx", None))
    return jax.shard_map(per_device, mesh=mesh, in_specs=in_specs, out_specs=out_specs, check_vma=False)
```

```python
import functools

import jax
import jax.numpy as jnp
from jax import lax
from jax.experimental import pallas as pl
from jax.experimental.pallas import tpu as pltpu
from jax.sharding import PartitionSpec as P

HEAD_SIZE = 128
QUERY_HEADS = 32
KEY_VALUE_HEADS = 4
ROPE_BASE = 1000000.0
CORE, Y, NEAR = 1, 2, 4
GROUP = (0, CORE, NEAR, NEAR | CORE)
VMEM_LIMIT = 48 * 1024 * 1024
COST = 3
LOG2E = 1.4426950408889634
VM = pl.BlockSpec(memory_space=pltpu.VMEM)
SM = pl.BlockSpec(memory_space=pltpu.SMEM)


def swap(x, mask):
    n = lax.axis_size("ctx")
    return lax.ppermute(x, "ctx", [(i, i ^ mask) for i in range(n)])


def swap_rep(x, mask):
    n = lax.axis_size("rep")
    return lax.ppermute(x, "rep", [(i, i ^ mask) for i in range(n)])


class Cell:
    def __init__(self, value):
        self.v = value


def after(x, *cells):
    cells = [c for c in cells if c is not None]
    if not cells:
        return x
    results = lax.optimization_barrier((x, *[c.v for c in cells]))
    for c, v in zip(cells, results[1:]):
        c.v = v
    return results[0]


def gather_rep(x, axis):
    rep = lax.axis_index("rep")
    bit = 1
    while bit < lax.axis_size("rep"):
        other = swap_rep(x, bit)
        high = (rep & bit) != 0
        x = jnp.concatenate([jnp.where(high, other, x), jnp.where(high, x, other)], axis=axis)
        bit *= 2
    return x


def call(body, out_shape, specs, flops, nbytes, args, scratch=(), name=None):
    outs = tuple(out_shape)
    return pl.pallas_call(
        body,
        out_shape=outs,
        in_specs=specs,
        out_specs=tuple(VM for _ in outs),
        scratch_shapes=list(scratch),
        compiler_params=pltpu.CompilerParams(vmem_limit_bytes=VMEM_LIMIT),
        cost_estimate=pl.CostEstimate(flops=int(flops * COST), bytes_accessed=int(nbytes * COST), transcendentals=0),
        name=name,
    )(*args)


def norm_body(masks, place, tokens, gain, own, core, far):
    ctx, rep = place[0], place[1]
    rows, width = tokens.shape
    kb = own.shape[1] // len(masks)
    step = 32
    share = far.shape[0]

    def normed(part, out_part, targets):
        t = tokens[part, :].astype(jnp.float32)
        scale = lax.rsqrt(jnp.sum(t * t, axis=-1, keepdims=True) * (1.0 / width) + 1e-06)
        for e, ref, first in targets:
            for j, m in enumerate(masks):
                block = pl.ds(pl.multiple_of((ctx ^ (m | e)) * kb, 128), kb)
                v = tokens[part, block].astype(jnp.float32) * scale * gain[:, block].astype(jnp.float32)
                ref[out_part, first + j * kb : first + (j + 1) * kb] = v.astype(jnp.bfloat16)

    def distant(i, carry):
        part = pl.ds(pl.multiple_of(rep * share + i * step, step), step)
        normed(part, pl.ds(i * step, step), ((NEAR, far, 0), (NEAR | CORE, far, own.shape[1])))
        return carry

    def local(i, carry):
        part = pl.ds(i * step, step)
        normed(part, part, ((0, own, 0), (CORE, core, 0)))
        return carry

    lax.fori_loop(0, share // step, distant, 0)
    lax.fori_loop(0, rows // step, local, 0)


def times(a, weights, columns):
    kb = weights[0].shape[0]
    total = None
    for j, w in enumerate(weights):
        part = jnp.dot(a[:, j * kb : (j + 1) * kb], w[:, columns], preferred_element_type=jnp.float32)
        total = part if total is None else total + part
    return total


def kv_body(n_share, place, own, own_sibling, *refs):
    near, cross = refs[:n_share], refs[n_share : 2 * n_share]
    weights, (kept, sent) = refs[2 * n_share : -2], refs[-2:]
    half = len(weights) // 2
    rep = place[1]
    rows = own.shape[0]
    share = rows // n_share

    def product(here, there):
        return times(here, weights[:half], slice(None)) + times(there, weights[half:], slice(None))

    mine = product(own, own_sibling)
    kept[0:rows, :] = mine
    sent[rows : 2 * rows, :] = mine.astype(jnp.bfloat16)
    for far in range(n_share):
        start = pl.multiple_of((rep ^ far) * share, share)
        part = product(near[far], cross[far])
        kept[pl.ds(rows + start, share), :] = part
        sent[pl.ds(start, share), :] = part.astype(jnp.bfloat16)


def kv_finish_body(spread, place, kept, came, bias, cosine, sine, half, own):
    rows, width = own.shape
    near = (place[0] >> 2) & 1
    heads = width // (2 * HEAD_SIZE)

    def value(part, columns):
        total = kept[part, columns] + came[part, columns].astype(jnp.float32)
        return total + bias[:, columns].astype(jnp.float32)

    for i in range(2):
        part, table = slice(i * rows, (i + 1) * rows), slice(2 * i * rows, (2 * i + 1) * rows)
        for v in range(2):
            first = (v * heads + near * spread) * HEAD_SIZE
            x = value(part, pl.ds(pl.multiple_of(first, HEAD_SIZE), HEAD_SIZE))
            x = x if v else rotate(x, cosine[table, :], sine[table, :])
            half[part, v * HEAD_SIZE : (v + 1) * HEAD_SIZE] = x.astype(jnp.bfloat16)
    for h in range(2 * heads):
        columns = slice(h * HEAD_SIZE, (h + 1) * HEAD_SIZE)
        x = value(slice(0, rows), columns)
        x = x if h >= heads else rotate(x, cosine[:rows, :], sine[:rows, :])
        own[:, columns] = x.astype(jnp.bfloat16)


def join_body(n_share, place, own, core, *refs):
    near, cross, joined = refs[:n_share], refs[n_share : 2 * n_share], refs[-1]
    rep = place[1]
    rows = own.shape[0]
    share = rows // n_share
    joined[0:rows, :] = own[...]
    joined[rows : 2 * rows, :] = core[...]
    for i, parts in ((2, near), (3, cross)):
        for far, part in enumerate(parts):
            start = pl.multiple_of(i * rows + (rep ^ far) * share, share)
            joined[pl.ds(start, share), :] = part[...]


def query_body(place, joined, *refs):
    weights, (kept, sent) = refs[:-2], refs[-2:]
    core = place[0] & 1
    rows, half = joined.shape[0] // 4, kept.shape[1]
    mine = pl.ds(pl.multiple_of(core * half, 128), half)
    other = pl.ds(pl.multiple_of((1 - core) * half, 128), half)
    kept[...] = times(joined, weights, mine)
    product = times(joined, weights, other).astype(jnp.bfloat16)
    for i in range(4):
        turned = i ^ 1
        sent[turned * rows : (turned + 1) * rows, :] = product[i * rows : (i + 1) * rows, :]


def halve_body(place, kept, came, mine, sent):
    near = (place[0] >> 2) & 1
    n = mine.shape[1]
    half = mine.shape[0] // 2
    here = pl.ds(pl.multiple_of(near * n, 128), n)
    there = pl.ds(pl.multiple_of((1 - near) * n, 128), n)
    mine[...] = kept[:, here] + came[:, here].astype(jnp.float32)
    for i in range(2):
        rows, turned = slice(i * half, (i + 1) * half), slice((1 - i) * half, (2 - i) * half)
        sent[turned, :] = (kept[rows, there] + came[rows, there].astype(jnp.float32)).astype(jnp.bfloat16)


def rotate(v, cosine, sine):
    half = HEAD_SIZE // 2
    turned = jnp.concatenate([v[:, half:], v[:, :half]], axis=1)
    return v * cosine + turned * sine


def attend_body(n_bits, place, mine, other, bias, cosine, sine, cache, out, q, acc, top):
    ctx = place[0]
    rows4, width = mine.shape
    rows = rows4 // 4
    pair = 2 * rows
    heads = width // HEAD_SIZE
    tile = heads * pair
    for h in range(heads):
        cols = slice(h * HEAD_SIZE, (h + 1) * HEAD_SIZE)
        v = mine[:, cols] + other[:, cols].astype(jnp.float32) + bias[:, cols].astype(jnp.float32)
        v = rotate(v, cosine[...], sine[...]).astype(jnp.bfloat16)
        for f in range(2):
            q[f * tile + h * pair : f * tile + (h + 1) * pair, :] = v[f * pair : (f + 1) * pair, :]
    factor = LOG2E * HEAD_SIZE ** (-0.5)
    ones = jnp.ones((pair, HEAD_SIZE), jnp.bfloat16)

    def place_of(k):
        return (k >> 2) | ((k & 2) << (n_bits - 3)) | ((k & 1) << (n_bits - 1))

    def load(k, first):
        spots = [pl.ds(pl.multiple_of(place_of(b) * rows, 128), rows) for b in (k, k ^ 1)]
        return jnp.concatenate([cache[s, first : first + HEAD_SIZE] for s in spots], axis=0)

    def scores(part, k):
        return lax.dot_general(
            q[part, :], load(k, 0), (((1,), (1,)), ((), ())), preferred_element_type=jnp.float32
        )

    def weighted(s, m, k):
        p = jnp.exp2((s - jnp.concatenate([m] * (pair // HEAD_SIZE), axis=1)) * factor).astype(jnp.bfloat16)
        return jnp.dot(p, jnp.concatenate([load(k, HEAD_SIZE), ones], axis=1), preferred_element_type=jnp.float32)

    def begin(f):
        part = slice(f * tile, (f + 1) * tile)
        s = scores(part, NEAR * f)
        r = lax.broadcasted_iota(jnp.int32, s.shape, 0) % pair
        c = lax.broadcasted_iota(jnp.int32, s.shape, 1)
        odd = ctx & 1
        row = ((r // rows) ^ odd) * rows + r % rows
        col = ((c // rows) ^ odd) * rows + c % rows
        s = jnp.where(col <= row, s, -1e30)
        m = jnp.broadcast_to(jnp.max(s, axis=-1, keepdims=True), (tile, HEAD_SIZE))
        top[part, :] = m
        acc[part, :] = weighted(s, m, NEAR * f)

    def step(start, k):
        part = pl.ds(start, tile)
        s = scores(part, k)
        old = top[part, :]
        m = jnp.maximum(old, jnp.max(s, axis=-1, keepdims=True))
        top[part, :] = m
        shrink = jnp.exp2((old - m) * factor)
        acc[part, :] = acc[part, :] * jnp.concatenate([shrink, shrink], axis=1) + weighted(s, m, k)

    begin(0)
    begin(1)
    here, there = ctx >> 1, (ctx ^ NEAR) >> 1
    common = jnp.minimum(here, there)

    def both(b, carry):
        k = ctx ^ (2 * b)
        step(0, k)
        step(tile, k)
        return carry

    def single(b, carry):
        step(pl.multiple_of(jnp.where(here > there, 0, tile), 128), ctx ^ (2 * b))
        return carry

    lax.fori_loop(0, common, both, 0)
    lax.fori_loop(common, jnp.maximum(here, there), single, 0)
    for f in range(2):
        for h in range(heads):
            a = acc[f * tile + h * pair : f * tile + (h + 1) * pair, :]
            part = (a[:, :HEAD_SIZE] / a[:, HEAD_SIZE:]).astype(jnp.bfloat16)
            out[f * pair : (f + 1) * pair, h * HEAD_SIZE : (h + 1) * HEAD_SIZE] = part


def collect_body(n_parts, heads_each, place, *refs):
    pieces, out = refs[:-1], refs[-1]
    ctx, rep = place[0], place[1]
    rows = pieces[0].shape[0] // 4
    wide = pieces[0].shape[1]
    members = out.shape[0]
    size = rows // members
    for d, distance in enumerate(GROUP):
        owner = ctx ^ distance
        group = ((owner >> 2) & 1) * 2 + (owner & 1)
        for i in range(n_parts):
            piece = pieces[d * n_parts + i]
            column = pl.ds(pl.multiple_of(group * (n_parts * wide) + i * wide, 128), wide)
            for far in range(members):
                for e in range(4):
                    part = pl.ds(pl.multiple_of((e ^ d) * rows + (rep ^ far) * size, size), size)
                    out[far, e * size : (e + 1) * size, column] = piece[part, :]


def output_body(att, *refs):
    weights, out = refs[:-1], refs[-1]
    n = weights[0].shape[1]
    join = 2 if n < 256 and len(weights) % 2 == 0 else 1
    for far in range(att.shape[0]):
        for j in range(0, len(weights), join):
            w = jnp.concatenate([weights[j + i][...] for i in range(join)], axis=1)
            product = jnp.dot(att[far], w, preferred_element_type=jnp.float32)
            out[far, :, j * n : (j + join) * n] = product.astype(jnp.bfloat16)


def place_body(masks, n_sub, place, *refs):
    sums, fars, cores, out = refs[:n_sub], refs[n_sub : 2 * n_sub], refs[2 * n_sub : -1], refs[-1]
    ctx = place[0]
    size = out.shape[0]
    sub = sums[0].shape[1] // len(masks)
    for s in range(n_sub):
        sources = ((0, sums[s], 0), (NEAR, fars[s], 0), (CORE, cores[s], 0), (NEAR | CORE, cores[s], size))
        for e, ref, first in sources:
            for j, m in enumerate(masks):
                start = (ctx ^ (m | e)) * (sub * n_sub) + s * sub
                out[:, pl.ds(pl.multiple_of(start, 128), sub)] = ref[first : first + size, j * sub : (j + 1) * sub]


class Stream:
    def __init__(self):
        self.last = None

    def swap(self, x, mask, *cells):
        cells = [c for c in cells if c is not self.last]
        self.last = Cell(swap(after(x, self.last, *cells), mask))
        return self.last


def per_device(tokens, norm_gain, q_weight, q_bias, kv_weight, kv_bias, out_weight):
    rows, width = tokens.shape
    n_ctx, n_rep = lax.axis_size("ctx"), lax.axis_size("rep")
    n_bits = n_ctx.bit_length() - 1
    ctx, rep = lax.axis_index("ctx"), lax.axis_index("rep")
    place = jnp.stack([ctx, rep]).astype(jnp.int32)
    head_group = QUERY_HEADS // KEY_VALUE_HEADS
    local_heads = q_weight.shape[1] // HEAD_SIZE
    own_heads = local_heads // 4
    high_bits = [1 << b for b in range(3, n_bits)]
    masks = [0]
    for bit in high_bits + [Y]:
        masks = masks + [m | bit for m in masks]
    masks = sorted(masks)
    n_masks = len(masks)

    n_q = min(4, own_heads)
    heads = own_heads // n_q
    n = heads * HEAD_SIZE
    bias = q_bias.reshape(4, n_q, n)
    n_out = max(1, min(4, out_weight.shape[1] // 128))
    out_cols = out_weight.shape[1] // n_out
    kv_heads = max(1, local_heads // head_group)
    leading = rep * local_heads // head_group

    def heads_used(x):
        whole = gather_rep(x, x.ndim - 1)
        cuts = [(offset + leading) * HEAD_SIZE for offset in (0, KEY_VALUE_HEADS)]
        return jnp.concatenate(
            [lax.dynamic_slice_in_dim(whole, c, kv_heads * HEAD_SIZE, x.ndim - 1) for c in cuts], axis=-1
        )

    kv_weight, kv_bias = heads_used(kv_weight), heads_used(kv_bias)
    pieces = {"kv": kv_weight}
    for i in range(n_q):
        columns = [((z * 2 + c) * n_q + i) * n for c in range(2) for z in range(2)]
        pieces[f"q{i}"] = jnp.concatenate([q_weight[:, first : first + n] for first in columns], axis=1)
    for i in range(n_out):
        pieces[f"o{i}"] = out_weight[:, i * out_cols : (i + 1) * out_cols]
    blocks = {name: {0: Cell(piece)} for name, piece in pieces.items()}
    z_stream, own_stream, y_stream = Stream(), Stream(), Stream()

    def step(name):
        if name in blocks:
            before = (z_stream.last,) if name[0] == "o" else (z_stream.last, own_stream.last)
            for bit in high_bits:
                for m in sorted(blocks[name]):
                    blocks[name][m | bit] = z_stream.swap(blocks[name][m].v, bit, *before)
            blocks[name][Y] = own_stream.swap(blocks[name][0].v, Y, *before)

    def rest(name):
        if name in blocks:
            for m in sorted(blocks[name]):
                if m and not m & Y:
                    blocks[name][m | Y] = y_stream.swap(blocks[name][m].v, Y)

    def weights(name):
        return [blocks[name][m].v for m in masks]

    def z_of(name):
        return blocks[name][max(m for m in masks if not m & Y)] if name in blocks and high_bits else None

    def y_of(name):
        return blocks[name][Y] if name in blocks else None

    step("q0")
    step("kv")
    rest("q0")
    rest("kv")
    step("q1")
    step("q2")
    rest("q1")

    kw = width // 4
    share = rows // n_rep
    a_own, a_core, a_far = call(
        functools.partial(norm_body, masks),
        (
            jax.ShapeDtypeStruct((rows, kw), jnp.bfloat16),
            jax.ShapeDtypeStruct((rows, kw), jnp.bfloat16),
            jax.ShapeDtypeStruct((share, 2 * kw), jnp.bfloat16),
        ),
        [SM, VM, VM], 0, 3 * rows * width * 2, (place, tokens, norm_gain.reshape(1, width)), name="normed",
    )
    cross = swap(a_far[:, kw:], NEAR)
    near_share = swap(a_far[:, :kw], NEAR)
    cross = [cross] + [swap_rep(cross, far) for far in range(1, n_rep)]
    near_share = [near_share] + [swap_rep(near_share, far) for far in range(1, n_rep)]

    middle = HEAD_SIZE // 2
    exponent = jnp.arange(middle, dtype=jnp.float32) * (2.0 / HEAD_SIZE)
    starts = jnp.stack([(ctx ^ e) * rows for e in GROUP])
    positions = (starts[:, None] + jnp.arange(rows, dtype=jnp.int32)[None, :]).reshape(-1).astype(jnp.float32)
    angles = positions[:, None] * (ROPE_BASE ** (-exponent))[None, :]
    cosine, sine = jnp.cos(angles), jnp.sin(angles)
    cosine = jnp.concatenate([cosine, cosine], axis=1)
    sine = jnp.concatenate([-sine, sine], axis=1)

    kv_cols = kv_weight.shape[1]
    kv_blocks = weights("kv")
    kv_blocks += [swap(w, CORE) for w in kv_blocks]
    kept, sent = call(
        functools.partial(kv_body, n_rep),
        (
            jax.ShapeDtypeStruct((2 * rows, kv_cols), jnp.float32),
            jax.ShapeDtypeStruct((2 * rows, kv_cols), jnp.bfloat16),
        ),
        [SM] + [VM] * (2 + 2 * n_rep + 2 * n_masks), 8 * rows * kw * kv_cols, 4 * kw * (2 * rows + kv_cols),
        (place, a_own, a_core, *near_share, *cross, *kv_blocks), name="kv_project",
    )
    spread = local_heads // 2 // head_group
    cache, kv_own = call(
        functools.partial(kv_finish_body, spread),
        (
            jax.ShapeDtypeStruct((2 * rows, 2 * HEAD_SIZE), jnp.bfloat16),
            jax.ShapeDtypeStruct((rows, kv_cols), jnp.bfloat16),
        ),
        [SM] + [VM] * 5, 0, 14 * rows * kv_cols,
        (place, kept, swap(sent, NEAR), kv_bias.reshape(1, kv_cols), cosine, sine), name="kv_finish",
    )
    all_heads = gather_rep(kv_own, 1)
    ordered = []
    for v in range(2):
        for h in range(KEY_VALUE_HEADS):
            owner = h // kv_heads * (n_rep * kv_heads // KEY_VALUE_HEADS)
            first = owner * kv_cols + (v * kv_heads + h % kv_heads) * HEAD_SIZE
            ordered.append(all_heads[:, first : first + HEAD_SIZE])
    key_value_cache = jnp.concatenate(ordered, axis=1)
    (joined,) = call(
        functools.partial(join_body, n_rep), (jax.ShapeDtypeStruct((4 * rows, kw), jnp.bfloat16),),
        [SM] + [VM] * (2 + 2 * n_rep), 0, 16 * rows * kw,
        (place, a_own, swap(a_core, CORE), *near_share, *[swap(x, CORE) for x in cross]), name="joined",
    )
    near = (ctx >> 2) & 1

    rest("q2")
    came = []
    for bit in high_bits:
        came.append((cache, z_stream.swap(cache, bit)))
        cache = jnp.concatenate([cache, came[-1][1].v], axis=0)
    step("q3")
    cache = jnp.concatenate([came[-1][0], came[-1][1].v], axis=0)
    other = y_stream.swap(cache, Y)
    rest("q3")
    for i in range(n_out):
        step(f"o{i}")
        rest(f"o{i}")
    cache = jnp.concatenate([cache, other.v], axis=0)
    cache = jnp.concatenate([cache, swap(cache, CORE)], axis=0)

    n_tokens = rows * n_ctx
    own_bias = lax.dynamic_index_in_dim(bias, near * 2 + (ctx & 1), 0, keepdims=False)
    att = {d: [] for d in GROUP}
    for i in range(n_q):
        kept, sent = call(
            query_body,
            (
                jax.ShapeDtypeStruct((4 * rows, 2 * n), jnp.float32),
                jax.ShapeDtypeStruct((4 * rows, 2 * n), jnp.bfloat16),
            ),
            [SM] + [VM] * (1 + n_masks), 8 * rows * kw * 4 * n, 2 * kw * (4 * rows + 4 * n),
            (place, joined, *weights(f"q{i}")), name=f"q_project{i}",
        )
        mine, sent = call(
            halve_body,
            (jax.ShapeDtypeStruct((4 * rows, n), jnp.float32), jax.ShapeDtypeStruct((4 * rows, n), jnp.bfloat16)),
            [SM, VM, VM], 0, 4 * rows * n * 18, (place, kept, swap(sent, CORE)), name=f"q_halve{i}",
        )
        (attended,) = call(
            functools.partial(attend_body, n_bits),
            (jax.ShapeDtypeStruct((4 * rows, n), jnp.bfloat16),),
            [SM] + [VM] * 6, 4 * heads * 4 * rows * n_tokens * HEAD_SIZE * 2, 2 * n_tokens * HEAD_SIZE * 2,
            (place, mine, swap(sent, NEAR), own_bias[i : i + 1], cosine, sine, cache),
            scratch=[
                pltpu.VMEM((4 * heads * rows, HEAD_SIZE), jnp.bfloat16),
                pltpu.VMEM((4 * heads * rows, 2 * HEAD_SIZE), jnp.float32),
                pltpu.VMEM((4 * heads * rows, HEAD_SIZE), jnp.float32),
            ],
            name=f"attend{i}",
        )
        far = swap(attended, NEAR)
        att[0].append(attended)
        att[NEAR].append(far)
        att[CORE].append(swap(attended, CORE))
        att[NEAR | CORE].append(swap(far, CORE))
    size = rows // n_rep
    (collected,) = call(
        functools.partial(collect_body, n_q, heads),
        (jax.ShapeDtypeStruct((n_rep, 4 * size, local_heads * HEAD_SIZE), jnp.bfloat16),),
        [SM] + [VM] * (4 * n_q), 0, 16 * rows * local_heads * HEAD_SIZE,
        (place, *[a for d in GROUP for a in att[d]]), name="collected",
    )

    sums, fars, cores = [], [], []
    for s in range(n_out):
        cols = out_cols * n_masks
        (partial,) = call(
            output_body,
            (jax.ShapeDtypeStruct((n_rep, 4 * size, cols), jnp.bfloat16),),
            [VM] * (1 + n_masks), 8 * rows * out_weight.shape[0] * cols,
            2 * out_weight.shape[0] * (4 * rows + cols) + 8 * rows * cols,
            (collected, *weights(f"o{s}")), name=f"out_project{s}",
        )
        total = partial[0].astype(jnp.float32)
        for far in range(1, n_rep):
            total = total + swap_rep(partial[far], far).astype(jnp.float32)
        total = total.astype(jnp.bfloat16)
        came = swap(total[2 * size :], NEAR)
        sums.append(total)
        fars.append(came)
        cores.append(swap(jnp.concatenate([total[size : 2 * size], came[size:]], axis=0), CORE))
    (result,) = call(
        functools.partial(place_body, masks, n_out),
        (jax.ShapeDtypeStruct((size, width), jnp.bfloat16),),
        [SM] + [VM] * (3 * n_out), 0, 2 * size * width * 2, (place, *sums, *fars, *cores), name="placed",
    )
    return result, key_value_cache


def solution(mesh):
    in_specs = (
        P("ctx", None),
        P(),
        P("ctx", "rep"),
        P("rep"),
        P("ctx", "rep"),
        P("rep"),
        P("rep", "ctx"),
    )
    out_specs = (P(("ctx", "rep"), None), P("ctx", None))
    return jax.shard_map(per_device, mesh=mesh, in_specs=in_specs, out_specs=out_specs, check_vma=False)
```

```python
import functools

import jax
import jax.numpy as jnp
from jax import lax
from jax.experimental import pallas as pl
from jax.experimental.pallas import tpu as pltpu
from jax.sharding import PartitionSpec as P

HEAD_SIZE = 128
QUERY_HEADS = 32
KEY_VALUE_HEADS = 4
ROPE_BASE = 1000000.0
CORE, Y, NEAR = 1, 2, 4
GROUP = (0, CORE, NEAR, NEAR | CORE)
VMEM_LIMIT = 48 * 1024 * 1024
COST = 4
LOG2E = 1.4426950408889634
VM = pl.BlockSpec(memory_space=pltpu.VMEM)
SM = pl.BlockSpec(memory_space=pltpu.SMEM)


def swap(x, mask):
    n = lax.axis_size("ctx")
    return lax.ppermute(x, "ctx", [(i, i ^ mask) for i in range(n)])


def swap_rep(x, mask):
    n = lax.axis_size("rep")
    return lax.ppermute(x, "rep", [(i, i ^ mask) for i in range(n)])


class Cell:
    def __init__(self, value):
        self.v = value


def after(x, *cells):
    cells = [c for c in cells if c is not None]
    if not cells:
        return x
    results = lax.optimization_barrier((x, *[c.v for c in cells]))
    for c, v in zip(cells, results[1:]):
        c.v = v
    return results[0]


def gather_rep(x, axis):
    rep = lax.axis_index("rep")
    bit = 1
    while bit < lax.axis_size("rep"):
        other = swap_rep(x, bit)
        high = (rep & bit) != 0
        x = jnp.concatenate([jnp.where(high, other, x), jnp.where(high, x, other)], axis=axis)
        bit *= 2
    return x


def call(body, out_shape, specs, flops, nbytes, args, scratch=(), name=None):
    outs = tuple(out_shape)
    return pl.pallas_call(
        body,
        out_shape=outs,
        in_specs=specs,
        out_specs=tuple(VM for _ in outs),
        scratch_shapes=list(scratch),
        compiler_params=pltpu.CompilerParams(vmem_limit_bytes=VMEM_LIMIT),
        cost_estimate=pl.CostEstimate(flops=int(flops * COST), bytes_accessed=int(nbytes * COST), transcendentals=0),
        name=name,
    )(*args)


def norm_body(masks, place, tokens, gain, own, core, far):
    ctx, rep = place[0], place[1]
    rows, width = tokens.shape
    kb = own.shape[1] // len(masks)
    step = 32
    share = far.shape[0]

    def normed(part, out_part, targets):
        t = tokens[part, :].astype(jnp.float32)
        scale = lax.rsqrt(jnp.sum(t * t, axis=-1, keepdims=True) * (1.0 / width) + 1e-06)
        for e, ref, first in targets:
            for j, m in enumerate(masks):
                block = pl.ds(pl.multiple_of((ctx ^ (m | e)) * kb, 128), kb)
                v = tokens[part, block].astype(jnp.float32) * scale * gain[:, block].astype(jnp.float32)
                ref[out_part, first + j * kb : first + (j + 1) * kb] = v.astype(jnp.bfloat16)

    def distant(i, carry):
        part = pl.ds(pl.multiple_of(rep * share + i * step, step), step)
        normed(part, pl.ds(i * step, step), ((NEAR, far, 0), (NEAR | CORE, far, own.shape[1])))
        return carry

    def local(i, carry):
        part = pl.ds(i * step, step)
        normed(part, part, ((0, own, 0), (CORE, core, 0)))
        return carry

    lax.fori_loop(0, share // step, distant, 0)
    lax.fori_loop(0, rows // step, local, 0)


def times(a, weights, columns):
    kb = weights[0].shape[0]
    total = None
    for j, w in enumerate(weights):
        part = jnp.dot(a[:, j * kb : (j + 1) * kb], w[:, columns], preferred_element_type=jnp.float32)
        total = part if total is None else total + part
    return total


def kv_body(n_share, place, own, own_sibling, *refs):
    near, cross = refs[:n_share], refs[n_share : 2 * n_share]
    weights, (kept, sent) = refs[2 * n_share : -2], refs[-2:]
    half = len(weights) // 2
    rep = place[1]
    rows = own.shape[0]
    share = rows // n_share

    def product(here, there):
        return times(here, weights[:half], slice(None)) + times(there, weights[half:], slice(None))

    mine = product(own, own_sibling)
    kept[0:rows, :] = mine
    sent[rows : 2 * rows, :] = mine.astype(jnp.bfloat16)
    for far in range(n_share):
        start = pl.multiple_of((rep ^ far) * share, share)
        part = product(near[far], cross[far])
        kept[pl.ds(rows + start, share), :] = part
        sent[pl.ds(start, share), :] = part.astype(jnp.bfloat16)


def kv_finish_body(spread, place, kept, came, bias, cosine, sine, half, own):
    rows, width = own.shape
    near = (place[0] >> 2) & 1
    heads = width // (2 * HEAD_SIZE)

    def value(part, columns):
        total = kept[part, columns] + came[part, columns].astype(jnp.float32)
        return total + bias[:, columns].astype(jnp.float32)

    for i in range(2):
        part, table = slice(i * rows, (i + 1) * rows), slice(2 * i * rows, (2 * i + 1) * rows)
        for v in range(2):
            first = (v * heads + near * spread) * HEAD_SIZE
            x = value(part, pl.ds(pl.multiple_of(first, HEAD_SIZE), HEAD_SIZE))
            x = x if v else rotate(x, cosine[table, :], sine[table, :])
            half[part, v * HEAD_SIZE : (v + 1) * HEAD_SIZE] = x.astype(jnp.bfloat16)
    for h in range(2 * heads):
        columns = slice(h * HEAD_SIZE, (h + 1) * HEAD_SIZE)
        x = value(slice(0, rows), columns)
        x = x if h >= heads else rotate(x, cosine[:rows, :], sine[:rows, :])
        own[:, columns] = x.astype(jnp.bfloat16)


def join_body(n_share, place, own, core, *refs):
    near, cross, joined = refs[:n_share], refs[n_share : 2 * n_share], refs[-1]
    rep = place[1]
    rows = own.shape[0]
    share = rows // n_share
    joined[0:rows, :] = own[...]
    joined[rows : 2 * rows, :] = core[...]
    for i, parts in ((2, near), (3, cross)):
        for far, part in enumerate(parts):
            start = pl.multiple_of(i * rows + (rep ^ far) * share, share)
            joined[pl.ds(start, share), :] = part[...]


def query_body(place, joined, *refs):
    weights, (kept, sent) = refs[:-2], refs[-2:]
    core = place[0] & 1
    rows, half = joined.shape[0] // 4, kept.shape[1]
    mine = pl.ds(pl.multiple_of(core * half, 128), half)
    other = pl.ds(pl.multiple_of((1 - core) * half, 128), half)
    kept[...] = times(joined, weights, mine)
    product = times(joined, weights, other).astype(jnp.bfloat16)
    for i in range(4):
        turned = i ^ 1
        sent[turned * rows : (turned + 1) * rows, :] = product[i * rows : (i + 1) * rows, :]


def halve_body(place, kept, came, mine, sent):
    near = (place[0] >> 2) & 1
    n = mine.shape[1]
    half = mine.shape[0] // 2
    here = pl.ds(pl.multiple_of(near * n, 128), n)
    there = pl.ds(pl.multiple_of((1 - near) * n, 128), n)
    mine[...] = kept[:, here] + came[:, here].astype(jnp.float32)
    for i in range(2):
        rows, turned = slice(i * half, (i + 1) * half), slice((1 - i) * half, (2 - i) * half)
        sent[turned, :] = (kept[rows, there] + came[rows, there].astype(jnp.float32)).astype(jnp.bfloat16)


def rotate(v, cosine, sine):
    half = HEAD_SIZE // 2
    turned = jnp.concatenate([v[:, half:], v[:, :half]], axis=1)
    return v * cosine + turned * sine


def attend_body(n_bits, place, mine, other, bias, cosine, sine, cache, out, q, acc, top):
    ctx = place[0]
    rows4, width = mine.shape
    rows = rows4 // 4
    pair = 2 * rows
    heads = width // HEAD_SIZE
    tile = heads * pair
    for h in range(heads):
        cols = slice(h * HEAD_SIZE, (h + 1) * HEAD_SIZE)
        v = mine[:, cols] + other[:, cols].astype(jnp.float32) + bias[:, cols].astype(jnp.float32)
        v = rotate(v, cosine[...], sine[...]).astype(jnp.bfloat16)
        for f in range(2):
            q[f * tile + h * pair : f * tile + (h + 1) * pair, :] = v[f * pair : (f + 1) * pair, :]
    factor = LOG2E * HEAD_SIZE ** (-0.5)
    ones = jnp.ones((pair, HEAD_SIZE), jnp.bfloat16)

    def place_of(k):
        return (k >> 2) | ((k & 2) << (n_bits - 3)) | ((k & 1) << (n_bits - 1))

    def load(k, first):
        spots = [pl.ds(pl.multiple_of(place_of(b) * rows, 128), rows) for b in (k, k ^ 1)]
        return jnp.concatenate([cache[s, first : first + HEAD_SIZE] for s in spots], axis=0)

    def scores(part, k):
        return lax.dot_general(
            q[part, :], load(k, 0), (((1,), (1,)), ((), ())), preferred_element_type=jnp.float32
        )

    def weighted(s, m, k):
        p = jnp.exp2((s - jnp.concatenate([m] * (pair // HEAD_SIZE), axis=1)) * factor).astype(jnp.bfloat16)
        return jnp.dot(p, jnp.concatenate([load(k, HEAD_SIZE), ones], axis=1), preferred_element_type=jnp.float32)

    def begin(f):
        part = slice(f * tile, (f + 1) * tile)
        s = scores(part, NEAR * f)
        r = lax.broadcasted_iota(jnp.int32, s.shape, 0) % pair
        c = lax.broadcasted_iota(jnp.int32, s.shape, 1)
        odd = ctx & 1
        row = ((r // rows) ^ odd) * rows + r % rows
        col = ((c // rows) ^ odd) * rows + c % rows
        s = jnp.where(col <= row, s, -1e30)
        m = jnp.broadcast_to(jnp.max(s, axis=-1, keepdims=True), (tile, HEAD_SIZE))
        top[part, :] = m
        acc[part, :] = weighted(s, m, NEAR * f)

    def step(start, k):
        part = pl.ds(start, tile)
        s = scores(part, k)
        old = top[part, :]
        m = jnp.maximum(old, jnp.max(s, axis=-1, keepdims=True))
        top[part, :] = m
        shrink = jnp.exp2((old - m) * factor)
        acc[part, :] = acc[part, :] * jnp.concatenate([shrink, shrink], axis=1) + weighted(s, m, k)

    begin(0)
    begin(1)
    here, there = ctx >> 1, (ctx ^ NEAR) >> 1
    common = jnp.minimum(here, there)

    def both(b, carry):
        k = ctx ^ (2 * b)
        step(0, k)
        step(tile, k)
        return carry

    def single(b, carry):
        step(pl.multiple_of(jnp.where(here > there, 0, tile), 128), ctx ^ (2 * b))
        return carry

    lax.fori_loop(0, common, both, 0)
    lax.fori_loop(common, jnp.maximum(here, there), single, 0)
    for f in range(2):
        for h in range(heads):
            a = acc[f * tile + h * pair : f * tile + (h + 1) * pair, :]
            part = (a[:, :HEAD_SIZE] / a[:, HEAD_SIZE:]).astype(jnp.bfloat16)
            out[f * pair : (f + 1) * pair, h * HEAD_SIZE : (h + 1) * HEAD_SIZE] = part


def collect_body(n_parts, heads_each, place, *refs):
    pieces, out = refs[:-1], refs[-1]
    ctx, rep = place[0], place[1]
    rows = pieces[0].shape[0] // 4
    wide = pieces[0].shape[1]
    members = out.shape[0]
    size = rows // members
    for d, distance in enumerate(GROUP):
        owner = ctx ^ distance
        group = ((owner >> 2) & 1) * 2 + (owner & 1)
        for i in range(n_parts):
            piece = pieces[d * n_parts + i]
            column = pl.ds(pl.multiple_of(group * (n_parts * wide) + i * wide, 128), wide)
            for far in range(members):
                for e in range(4):
                    part = pl.ds(pl.multiple_of((e ^ d) * rows + (rep ^ far) * size, size), size)
                    out[far, e * size : (e + 1) * size, column] = piece[part, :]


def output_body(att, *refs):
    weights, out = refs[:-1], refs[-1]
    n = weights[0].shape[1]
    join = 2 if n < 256 and len(weights) % 2 == 0 else 1
    for far in range(att.shape[0]):
        for j in range(0, len(weights), join):
            w = jnp.concatenate([weights[j + i][...] for i in range(join)], axis=1)
            product = jnp.dot(att[far], w, preferred_element_type=jnp.float32)
            out[far, :, j * n : (j + join) * n] = product.astype(jnp.bfloat16)


def place_body(masks, n_sub, place, *refs):
    sums, fars, cores, out = refs[:n_sub], refs[n_sub : 2 * n_sub], refs[2 * n_sub : -1], refs[-1]
    ctx = place[0]
    size = out.shape[0]
    sub = sums[0].shape[1] // len(masks)
    for s in range(n_sub):
        sources = ((0, sums[s], 0), (NEAR, fars[s], 0), (CORE, cores[s], 0), (NEAR | CORE, cores[s], size))
        for e, ref, first in sources:
            for j, m in enumerate(masks):
                start = (ctx ^ (m | e)) * (sub * n_sub) + s * sub
                out[:, pl.ds(pl.multiple_of(start, 128), sub)] = ref[first : first + size, j * sub : (j + 1) * sub]


class Stream:
    def __init__(self):
        self.last = None

    def swap(self, x, mask, *cells):
        cells = [c for c in cells if c is not self.last]
        self.last = Cell(swap(after(x, self.last, *cells), mask))
        return self.last


def per_device(tokens, norm_gain, q_weight, q_bias, kv_weight, kv_bias, out_weight):
    rows, width = tokens.shape
    n_ctx, n_rep = lax.axis_size("ctx"), lax.axis_size("rep")
    n_bits = n_ctx.bit_length() - 1
    ctx, rep = lax.axis_index("ctx"), lax.axis_index("rep")
    place = jnp.stack([ctx, rep]).astype(jnp.int32)
    head_group = QUERY_HEADS // KEY_VALUE_HEADS
    local_heads = q_weight.shape[1] // HEAD_SIZE
    own_heads = local_heads // 4
    high_bits = [1 << b for b in range(3, n_bits)]
    masks = [0]
    for bit in high_bits + [Y]:
        masks = masks + [m | bit for m in masks]
    masks = sorted(masks)
    n_masks = len(masks)

    n_q = min(4, own_heads)
    heads = own_heads // n_q
    n = heads * HEAD_SIZE
    bias = q_bias.reshape(4, n_q, n)
    n_out = max(1, min(4, out_weight.shape[1] // 128))
    out_cols = out_weight.shape[1] // n_out
    kv_heads = max(1, local_heads // head_group)
    leading = rep * local_heads // head_group

    def heads_used(x):
        whole = gather_rep(x, x.ndim - 1)
        cuts = [(offset + leading) * HEAD_SIZE for offset in (0, KEY_VALUE_HEADS)]
        return jnp.concatenate(
            [lax.dynamic_slice_in_dim(whole, c, kv_heads * HEAD_SIZE, x.ndim - 1) for c in cuts], axis=-1
        )

    kv_weight, kv_bias = heads_used(kv_weight), heads_used(kv_bias)
    pieces = {"kv": kv_weight}
    for i in range(n_q):
        columns = [((z * 2 + c) * n_q + i) * n for c in range(2) for z in range(2)]
        pieces[f"q{i}"] = jnp.concatenate([q_weight[:, first : first + n] for first in columns], axis=1)
    for i in range(n_out):
        pieces[f"o{i}"] = out_weight[:, i * out_cols : (i + 1) * out_cols]
    blocks = {name: {0: Cell(piece)} for name, piece in pieces.items()}
    z_stream, own_stream, y_stream = Stream(), Stream(), Stream()

    def step(name):
        if name in blocks:
            before = (z_stream.last,) if name[0] == "o" else (z_stream.last, own_stream.last)
            for bit in high_bits:
                for m in sorted(blocks[name]):
                    blocks[name][m | bit] = z_stream.swap(blocks[name][m].v, bit, *before)
            blocks[name][Y] = own_stream.swap(blocks[name][0].v, Y, *before)

    def rest(name):
        if name in blocks:
            for m in sorted(blocks[name]):
                if m and not m & Y:
                    blocks[name][m | Y] = y_stream.swap(blocks[name][m].v, Y)

    def weights(name):
        return [blocks[name][m].v for m in masks]

    def z_of(name):
        return blocks[name][max(m for m in masks if not m & Y)] if name in blocks and high_bits else None

    def y_of(name):
        return blocks[name][Y] if name in blocks else None

    step("q0")
    step("kv")
    rest("q0")
    rest("kv")
    step("q1")
    step("q2")
    rest("q1")

    kw = width // 4
    share = rows // n_rep
    a_own, a_core, a_far = call(
        functools.partial(norm_body, masks),
        (
            jax.ShapeDtypeStruct((rows, kw), jnp.bfloat16),
            jax.ShapeDtypeStruct((rows, kw), jnp.bfloat16),
            jax.ShapeDtypeStruct((share, 2 * kw), jnp.bfloat16),
        ),
        [SM, VM, VM], 0, 3 * rows * width * 2, (place, tokens, norm_gain.reshape(1, width)), name="normed",
    )
    cross = swap(a_far[:, kw:], NEAR)
    near_share = swap(a_far[:, :kw], NEAR)
    cross = [cross] + [swap_rep(cross, far) for far in range(1, n_rep)]
    near_share = [near_share] + [swap_rep(near_share, far) for far in range(1, n_rep)]

    middle = HEAD_SIZE // 2
    exponent = jnp.arange(middle, dtype=jnp.float32) * (2.0 / HEAD_SIZE)
    starts = jnp.stack([(ctx ^ e) * rows for e in GROUP])
    positions = (starts[:, None] + jnp.arange(rows, dtype=jnp.int32)[None, :]).reshape(-1).astype(jnp.float32)
    angles = positions[:, None] * (ROPE_BASE ** (-exponent))[None, :]
    cosine, sine = jnp.cos(angles), jnp.sin(angles)
    cosine = jnp.concatenate([cosine, cosine], axis=1)
    sine = jnp.concatenate([-sine, sine], axis=1)

    kv_cols = kv_weight.shape[1]
    kv_blocks = weights("kv")
    kv_blocks += [swap(w, CORE) for w in kv_blocks]
    kept, sent = call(
        functools.partial(kv_body, n_rep),
        (
            jax.ShapeDtypeStruct((2 * rows, kv_cols), jnp.float32),
            jax.ShapeDtypeStruct((2 * rows, kv_cols), jnp.bfloat16),
        ),
        [SM] + [VM] * (2 + 2 * n_rep + 2 * n_masks), 8 * rows * kw * kv_cols, 4 * kw * (2 * rows + kv_cols),
        (place, a_own, a_core, *near_share, *cross, *kv_blocks), name="kv_project",
    )
    spread = local_heads // 2 // head_group
    cache, kv_own = call(
        functools.partial(kv_finish_body, spread),
        (
            jax.ShapeDtypeStruct((2 * rows, 2 * HEAD_SIZE), jnp.bfloat16),
            jax.ShapeDtypeStruct((rows, kv_cols), jnp.bfloat16),
        ),
        [SM] + [VM] * 5, 0, 14 * rows * kv_cols,
        (place, kept, swap(sent, NEAR), kv_bias.reshape(1, kv_cols), cosine, sine), name="kv_finish",
    )
    all_heads = gather_rep(kv_own, 1)
    ordered = []
    for v in range(2):
        for h in range(KEY_VALUE_HEADS):
            owner = h // kv_heads * (n_rep * kv_heads // KEY_VALUE_HEADS)
            first = owner * kv_cols + (v * kv_heads + h % kv_heads) * HEAD_SIZE
            ordered.append(all_heads[:, first : first + HEAD_SIZE])
    key_value_cache = jnp.concatenate(ordered, axis=1)
    (joined,) = call(
        functools.partial(join_body, n_rep), (jax.ShapeDtypeStruct((4 * rows, kw), jnp.bfloat16),),
        [SM] + [VM] * (2 + 2 * n_rep), 0, 16 * rows * kw,
        (place, a_own, swap(a_core, CORE), *near_share, *[swap(x, CORE) for x in cross]), name="joined",
    )
    near = (ctx >> 2) & 1

    rest("q2")
    came = []
    for bit in high_bits:
        came.append((cache, z_stream.swap(cache, bit)))
        cache = jnp.concatenate([cache, came[-1][1].v], axis=0)
    step("q3")
    cache = jnp.concatenate([came[-1][0], came[-1][1].v], axis=0)
    other = y_stream.swap(cache, Y)
    rest("q3")
    for i in range(n_out):
        step(f"o{i}")
        rest(f"o{i}")
    cache = jnp.concatenate([cache, other.v], axis=0)
    cache = jnp.concatenate([cache, swap(cache, CORE)], axis=0)

    n_tokens = rows * n_ctx
    own_bias = lax.dynamic_index_in_dim(bias, near * 2 + (ctx & 1), 0, keepdims=False)
    att = {d: [] for d in GROUP}
    for i in range(n_q):
        kept, sent = call(
            query_body,
            (
                jax.ShapeDtypeStruct((4 * rows, 2 * n), jnp.float32),
                jax.ShapeDtypeStruct((4 * rows, 2 * n), jnp.bfloat16),
            ),
            [SM] + [VM] * (1 + n_masks), 8 * rows * kw * 4 * n, 2 * kw * (4 * rows + 4 * n),
            (place, joined, *weights(f"q{i}")), name=f"q_project{i}",
        )
        mine, sent = call(
            halve_body,
            (jax.ShapeDtypeStruct((4 * rows, n), jnp.float32), jax.ShapeDtypeStruct((4 * rows, n), jnp.bfloat16)),
            [SM, VM, VM], 0, 4 * rows * n * 18, (place, kept, swap(sent, CORE)), name=f"q_halve{i}",
        )
        (attended,) = call(
            functools.partial(attend_body, n_bits),
            (jax.ShapeDtypeStruct((4 * rows, n), jnp.bfloat16),),
            [SM] + [VM] * 6, 4 * heads * 4 * rows * n_tokens * HEAD_SIZE * 2, 2 * n_tokens * HEAD_SIZE * 2,
            (place, mine, swap(sent, NEAR), own_bias[i : i + 1], cosine, sine, cache),
            scratch=[
                pltpu.VMEM((4 * heads * rows, HEAD_SIZE), jnp.bfloat16),
                pltpu.VMEM((4 * heads * rows, 2 * HEAD_SIZE), jnp.float32),
                pltpu.VMEM((4 * heads * rows, HEAD_SIZE), jnp.float32),
            ],
            name=f"attend{i}",
        )
        far = swap(attended, NEAR)
        att[0].append(attended)
        att[NEAR].append(far)
        att[CORE].append(swap(attended, CORE))
        att[NEAR | CORE].append(swap(far, CORE))
    size = rows // n_rep
    (collected,) = call(
        functools.partial(collect_body, n_q, heads),
        (jax.ShapeDtypeStruct((n_rep, 4 * size, local_heads * HEAD_SIZE), jnp.bfloat16),),
        [SM] + [VM] * (4 * n_q), 0, 16 * rows * local_heads * HEAD_SIZE,
        (place, *[a for d in GROUP for a in att[d]]), name="collected",
    )

    sums, fars, cores = [], [], []
    for s in range(n_out):
        cols = out_cols * n_masks
        (partial,) = call(
            output_body,
            (jax.ShapeDtypeStruct((n_rep, 4 * size, cols), jnp.bfloat16),),
            [VM] * (1 + n_masks), 8 * rows * out_weight.shape[0] * cols,
            2 * out_weight.shape[0] * (4 * rows + cols) + 8 * rows * cols,
            (collected, *weights(f"o{s}")), name=f"out_project{s}",
        )
        total = partial[0].astype(jnp.float32)
        for far in range(1, n_rep):
            total = total + swap_rep(partial[far], far).astype(jnp.float32)
        total = total.astype(jnp.bfloat16)
        came = swap(total[2 * size :], NEAR)
        sums.append(total)
        fars.append(came)
        cores.append(swap(jnp.concatenate([total[size : 2 * size], came[size:]], axis=0), CORE))
    (result,) = call(
        functools.partial(place_body, masks, n_out),
        (jax.ShapeDtypeStruct((size, width), jnp.bfloat16),),
        [SM] + [VM] * (3 * n_out), 0, 2 * size * width * 2, (place, *sums, *fars, *cores), name="placed",
    )
    return result, key_value_cache


def solution(mesh):
    in_specs = (
        P("ctx", None),
        P(),
        P("ctx", "rep"),
        P("rep"),
        P("ctx", "rep"),
        P("rep"),
        P("rep", "ctx"),
    )
    out_specs = (P(("ctx", "rep"), None), P("ctx", None))
    return jax.shard_map(per_device, mesh=mesh, in_specs=in_specs, out_specs=out_specs, check_vma=False)
```

```python
import functools

import jax
import jax.numpy as jnp
from jax import lax
from jax.experimental import pallas as pl
from jax.experimental.pallas import tpu as pltpu
from jax.sharding import PartitionSpec as P

HEAD_SIZE = 128
QUERY_HEADS = 32
KEY_VALUE_HEADS = 4
ROPE_BASE = 1000000.0
CORE, Y, NEAR = 1, 2, 4
GROUP = (0, CORE, NEAR, NEAR | CORE)
VMEM_LIMIT = 48 * 1024 * 1024
COST = 4
LOG2E = 1.4426950408889634
VM = pl.BlockSpec(memory_space=pltpu.VMEM)
SM = pl.BlockSpec(memory_space=pltpu.SMEM)


def swap(x, mask):
    n = lax.axis_size("ctx")
    return lax.ppermute(x, "ctx", [(i, i ^ mask) for i in range(n)])


def swap_rep(x, mask):
    n = lax.axis_size("rep")
    return lax.ppermute(x, "rep", [(i, i ^ mask) for i in range(n)])


class Cell:
    def __init__(self, value):
        self.v = value


def after(x, *cells):
    cells = [c for c in cells if c is not None]
    if not cells:
        return x
    results = lax.optimization_barrier((x, *[c.v for c in cells]))
    for c, v in zip(cells, results[1:]):
        c.v = v
    return results[0]


def gather_rep(x, axis):
    rep = lax.axis_index("rep")
    bit = 1
    while bit < lax.axis_size("rep"):
        other = swap_rep(x, bit)
        high = (rep & bit) != 0
        x = jnp.concatenate([jnp.where(high, other, x), jnp.where(high, x, other)], axis=axis)
        bit *= 2
    return x


def call(body, out_shape, specs, flops, nbytes, args, scratch=(), name=None):
    outs = tuple(out_shape)
    return pl.pallas_call(
        body,
        out_shape=outs,
        in_specs=specs,
        out_specs=tuple(VM for _ in outs),
        scratch_shapes=list(scratch),
        compiler_params=pltpu.CompilerParams(vmem_limit_bytes=VMEM_LIMIT),
        cost_estimate=pl.CostEstimate(flops=int(flops * COST), bytes_accessed=int(nbytes * COST), transcendentals=0),
        name=name,
    )(*args)


def norm_body(masks, place, tokens, gain, own, core, far):
    ctx, rep = place[0], place[1]
    rows, width = tokens.shape
    kb = own.shape[1] // len(masks)
    step = 32
    share = far.shape[0]

    def normed(part, out_part, targets):
        t = tokens[part, :].astype(jnp.float32)
        scale = lax.rsqrt(jnp.sum(t * t, axis=-1, keepdims=True) * (1.0 / width) + 1e-06)
        for e, ref, first in targets:
            for j, m in enumerate(masks):
                block = pl.ds(pl.multiple_of((ctx ^ (m | e)) * kb, 128), kb)
                v = tokens[part, block].astype(jnp.float32) * scale * gain[:, block].astype(jnp.float32)
                ref[out_part, first + j * kb : first + (j + 1) * kb] = v.astype(jnp.bfloat16)

    def distant(i, carry):
        part = pl.ds(pl.multiple_of(rep * share + i * step, step), step)
        normed(part, pl.ds(i * step, step), ((NEAR, far, 0), (NEAR | CORE, far, own.shape[1])))
        return carry

    def local(i, carry):
        part = pl.ds(i * step, step)
        normed(part, part, ((0, own, 0), (CORE, core, 0)))
        return carry

    lax.fori_loop(0, share // step, distant, 0)
    lax.fori_loop(0, rows // step, local, 0)


def times(a, weights, columns):
    kb = weights[0].shape[0]
    total = None
    for j, w in enumerate(weights):
        part = jnp.dot(a[:, j * kb : (j + 1) * kb], w[:, columns], preferred_element_type=jnp.float32)
        total = part if total is None else total + part
    return total


def kv_body(n_share, place, own, own_sibling, *refs):
    near, cross = refs[:n_share], refs[n_share : 2 * n_share]
    weights, (kept, sent) = refs[2 * n_share : -2], refs[-2:]
    half = len(weights) // 2
    rep = place[1]
    rows = own.shape[0]
    share = rows // n_share

    def product(here, there):
        return times(here, weights[:half], slice(None)) + times(there, weights[half:], slice(None))

    mine = product(own, own_sibling)
    kept[0:rows, :] = mine
    sent[rows : 2 * rows, :] = mine.astype(jnp.bfloat16)
    for far in range(n_share):
        start = pl.multiple_of((rep ^ far) * share, share)
        part = product(near[far], cross[far])
        kept[pl.ds(rows + start, share), :] = part
        sent[pl.ds(start, share), :] = part.astype(jnp.bfloat16)


def kv_finish_body(spread, place, kept, came, bias, cosine, sine, half, own):
    rows, width = own.shape
    near = (place[0] >> 2) & 1
    heads = width // (2 * HEAD_SIZE)

    def value(part, columns):
        total = kept[part, columns] + came[part, columns].astype(jnp.float32)
        return total + bias[:, columns].astype(jnp.float32)

    for i in range(2):
        part, table = slice(i * rows, (i + 1) * rows), slice(2 * i * rows, (2 * i + 1) * rows)
        for v in range(2):
            first = (v * heads + near * spread) * HEAD_SIZE
            x = value(part, pl.ds(pl.multiple_of(first, HEAD_SIZE), HEAD_SIZE))
            x = x if v else rotate(x, cosine[table, :], sine[table, :])
            half[part, v * HEAD_SIZE : (v + 1) * HEAD_SIZE] = x.astype(jnp.bfloat16)
    for h in range(2 * heads):
        columns = slice(h * HEAD_SIZE, (h + 1) * HEAD_SIZE)
        x = value(slice(0, rows), columns)
        x = x if h >= heads else rotate(x, cosine[:rows, :], sine[:rows, :])
        own[:, columns] = x.astype(jnp.bfloat16)


def join_body(n_share, place, own, core, *refs):
    near, cross, joined = refs[:n_share], refs[n_share : 2 * n_share], refs[-1]
    rep = place[1]
    rows = own.shape[0]
    share = rows // n_share
    joined[0:rows, :] = own[...]
    joined[rows : 2 * rows, :] = core[...]
    for i, parts in ((2, near), (3, cross)):
        for far, part in enumerate(parts):
            start = pl.multiple_of(i * rows + (rep ^ far) * share, share)
            joined[pl.ds(start, share), :] = part[...]


def query_body(place, joined, *refs):
    weights, (kept, sent) = refs[:-2], refs[-2:]
    core = place[0] & 1
    rows, half = joined.shape[0] // 4, kept.shape[1]
    mine = pl.ds(pl.multiple_of(core * half, 128), half)
    other = pl.ds(pl.multiple_of((1 - core) * half, 128), half)
    kept[...] = times(joined, weights, mine)
    product = times(joined, weights, other).astype(jnp.bfloat16)
    for i in range(4):
        turned = i ^ 1
        sent[turned * rows : (turned + 1) * rows, :] = product[i * rows : (i + 1) * rows, :]


def halve_body(place, kept, came, mine, sent):
    near = (place[0] >> 2) & 1
    n = mine.shape[1]
    half = mine.shape[0] // 2
    here = pl.ds(pl.multiple_of(near * n, 128), n)
    there = pl.ds(pl.multiple_of((1 - near) * n, 128), n)
    mine[...] = kept[:, here] + came[:, here].astype(jnp.float32)
    for i in range(2):
        rows, turned = slice(i * half, (i + 1) * half), slice((1 - i) * half, (2 - i) * half)
        sent[turned, :] = (kept[rows, there] + came[rows, there].astype(jnp.float32)).astype(jnp.bfloat16)


def rotate(v, cosine, sine):
    half = HEAD_SIZE // 2
    turned = jnp.concatenate([v[:, half:], v[:, :half]], axis=1)
    return v * cosine + turned * sine


def attend_body(n_bits, place, mine, other, bias, cosine, sine, cache, out, q, acc, top):
    ctx = place[0]
    rows4, width = mine.shape
    rows = rows4 // 4
    pair = 2 * rows
    heads = width // HEAD_SIZE
    tile = heads * pair
    for h in range(heads):
        cols = slice(h * HEAD_SIZE, (h + 1) * HEAD_SIZE)
        v = mine[:, cols] + other[:, cols].astype(jnp.float32) + bias[:, cols].astype(jnp.float32)
        v = rotate(v, cosine[...], sine[...]).astype(jnp.bfloat16)
        for f in range(2):
            q[f * tile + h * pair : f * tile + (h + 1) * pair, :] = v[f * pair : (f + 1) * pair, :]
    factor = LOG2E * HEAD_SIZE ** (-0.5)
    ones = jnp.ones((pair, HEAD_SIZE), jnp.bfloat16)

    def place_of(k):
        return (k >> 2) | ((k & 2) << (n_bits - 3)) | ((k & 1) << (n_bits - 1))

    def load(k, first):
        spots = [pl.ds(pl.multiple_of(place_of(b) * rows, 128), rows) for b in (k, k ^ 1)]
        return jnp.concatenate([cache[s, first : first + HEAD_SIZE] for s in spots], axis=0)

    def scores(part, k):
        return lax.dot_general(
            q[part, :], load(k, 0), (((1,), (1,)), ((), ())), preferred_element_type=jnp.float32
        )

    def weighted(s, m, k):
        p = jnp.exp2((s - jnp.concatenate([m] * (pair // HEAD_SIZE), axis=1)) * factor).astype(jnp.bfloat16)
        return jnp.dot(p, jnp.concatenate([load(k, HEAD_SIZE), ones], axis=1), preferred_element_type=jnp.float32)

    def begin(f):
        part = slice(f * tile, (f + 1) * tile)
        s = scores(part, NEAR * f)
        r = lax.broadcasted_iota(jnp.int32, s.shape, 0) % pair
        c = lax.broadcasted_iota(jnp.int32, s.shape, 1)
        odd = ctx & 1
        row = ((r // rows) ^ odd) * rows + r % rows
        col = ((c // rows) ^ odd) * rows + c % rows
        s = jnp.where(col <= row, s, -1e30)
        m = jnp.broadcast_to(jnp.max(s, axis=-1, keepdims=True), (tile, HEAD_SIZE))
        top[part, :] = m
        acc[part, :] = weighted(s, m, NEAR * f)

    def step(start, k):
        part = pl.ds(start, tile)
        s = scores(part, k)
        old = top[part, :]
        m = jnp.maximum(old, jnp.max(s, axis=-1, keepdims=True))
        top[part, :] = m
        shrink = jnp.exp2((old - m) * factor)
        acc[part, :] = acc[part, :] * jnp.concatenate([shrink, shrink], axis=1) + weighted(s, m, k)

    begin(0)
    begin(1)
    here, there = ctx >> 1, (ctx ^ NEAR) >> 1
    common = jnp.minimum(here, there)

    def both(b, carry):
        k = ctx ^ (2 * b)
        step(0, k)
        step(tile, k)
        return carry

    def single(b, carry):
        step(pl.multiple_of(jnp.where(here > there, 0, tile), 128), ctx ^ (2 * b))
        return carry

    lax.fori_loop(0, common, both, 0)
    lax.fori_loop(common, jnp.maximum(here, there), single, 0)
    for f in range(2):
        for h in range(heads):
            a = acc[f * tile + h * pair : f * tile + (h + 1) * pair, :]
            part = (a[:, :HEAD_SIZE] / a[:, HEAD_SIZE:]).astype(jnp.bfloat16)
            out[f * pair : (f + 1) * pair, h * HEAD_SIZE : (h + 1) * HEAD_SIZE] = part


def collect_body(n_parts, heads_each, place, *refs):
    pieces, out = refs[:-1], refs[-1]
    ctx, rep = place[0], place[1]
    rows = pieces[0].shape[0] // 4
    wide = pieces[0].shape[1]
    members = out.shape[0]
    size = rows // members
    for d, distance in enumerate(GROUP):
        owner = ctx ^ distance
        group = ((owner >> 2) & 1) * 2 + (owner & 1)
        for i in range(n_parts):
            piece = pieces[d * n_parts + i]
            column = pl.ds(pl.multiple_of(group * (n_parts * wide) + i * wide, 128), wide)
            for far in range(members):
                for e in range(4):
                    part = pl.ds(pl.multiple_of((e ^ d) * rows + (rep ^ far) * size, size), size)
                    out[far, e * size : (e + 1) * size, column] = piece[part, :]


def output_body(att, *refs):
    weights, out = refs[:-1], refs[-1]
    n = weights[0].shape[1]
    join = 2 if n < 256 and len(weights) % 2 == 0 else 1
    for far in range(att.shape[0]):
        for j in range(0, len(weights), join):
            w = jnp.concatenate([weights[j + i][...] for i in range(join)], axis=1)
            product = jnp.dot(att[far], w, preferred_element_type=jnp.float32)
            out[far, :, j * n : (j + join) * n] = product.astype(jnp.bfloat16)


def place_body(masks, n_sub, place, *refs):
    sums, fars, cores, crosses = (refs[i * n_sub : (i + 1) * n_sub] for i in range(4))
    out = refs[-1]
    ctx = place[0]
    size = out.shape[0]
    sub = sums[0].shape[1] // len(masks)
    for s in range(n_sub):
        sources = ((0, sums[s], 0), (NEAR, fars[s], 0), (CORE, cores[s], 0), (NEAR | CORE, crosses[s], 0))
        for e, ref, first in sources:
            for j, m in enumerate(masks):
                start = (ctx ^ (m | e)) * (sub * n_sub) + s * sub
                out[:, pl.ds(pl.multiple_of(start, 128), sub)] = ref[first : first + size, j * sub : (j + 1) * sub]


class Stream:
    def __init__(self):
        self.last = None

    def swap(self, x, mask, *cells):
        cells = [c for c in cells if c is not self.last]
        self.last = Cell(swap(after(x, self.last, *cells), mask))
        return self.last


def per_device(tokens, norm_gain, q_weight, q_bias, kv_weight, kv_bias, out_weight):
    rows, width = tokens.shape
    n_ctx, n_rep = lax.axis_size("ctx"), lax.axis_size("rep")
    n_bits = n_ctx.bit_length() - 1
    ctx, rep = lax.axis_index("ctx"), lax.axis_index("rep")
    place = jnp.stack([ctx, rep]).astype(jnp.int32)
    head_group = QUERY_HEADS // KEY_VALUE_HEADS
    local_heads = q_weight.shape[1] // HEAD_SIZE
    own_heads = local_heads // 4
    high_bits = [1 << b for b in range(3, n_bits)]
    masks = [0]
    for bit in high_bits + [Y]:
        masks = masks + [m | bit for m in masks]
    masks = sorted(masks)
    n_masks = len(masks)

    n_q = min(4, own_heads)
    heads = own_heads // n_q
    n = heads * HEAD_SIZE
    bias = q_bias.reshape(4, n_q, n)
    n_out = max(1, min(4, out_weight.shape[1] // 128))
    out_cols = out_weight.shape[1] // n_out
    kv_heads = max(1, local_heads // head_group)
    leading = rep * local_heads // head_group

    def heads_used(x):
        whole = gather_rep(x, x.ndim - 1)
        cuts = [(offset + leading) * HEAD_SIZE for offset in (0, KEY_VALUE_HEADS)]
        return jnp.concatenate(
            [lax.dynamic_slice_in_dim(whole, c, kv_heads * HEAD_SIZE, x.ndim - 1) for c in cuts], axis=-1
        )

    kv_weight, kv_bias = heads_used(kv_weight), heads_used(kv_bias)
    pieces = {"kv": kv_weight}
    for i in range(n_q):
        columns = [((z * 2 + c) * n_q + i) * n for c in range(2) for z in range(2)]
        pieces[f"q{i}"] = jnp.concatenate([q_weight[:, first : first + n] for first in columns], axis=1)
    for i in range(n_out):
        pieces[f"o{i}"] = out_weight[:, i * out_cols : (i + 1) * out_cols]
    blocks = {name: {0: Cell(piece)} for name, piece in pieces.items()}
    z_stream, own_stream, y_stream = Stream(), Stream(), Stream()

    def step(name):
        if name in blocks:
            before = (z_stream.last,) if name[0] == "o" else (z_stream.last, own_stream.last)
            for bit in high_bits:
                for m in sorted(blocks[name]):
                    blocks[name][m | bit] = z_stream.swap(blocks[name][m].v, bit, *before)
            blocks[name][Y] = own_stream.swap(blocks[name][0].v, Y, *before)

    def rest(name):
        if name in blocks:
            for m in sorted(blocks[name]):
                if m and not m & Y:
                    blocks[name][m | Y] = y_stream.swap(blocks[name][m].v, Y)

    def weights(name):
        return [blocks[name][m].v for m in masks]

    def z_of(name):
        return blocks[name][max(m for m in masks if not m & Y)] if name in blocks and high_bits else None

    def y_of(name):
        return blocks[name][Y] if name in blocks else None

    step("q0")
    step("kv")
    rest("q0")
    rest("kv")
    step("q1")
    step("q2")
    rest("q1")

    kw = width // 4
    share = rows // n_rep
    a_own, a_core, a_far = call(
        functools.partial(norm_body, masks),
        (
            jax.ShapeDtypeStruct((rows, kw), jnp.bfloat16),
            jax.ShapeDtypeStruct((rows, kw), jnp.bfloat16),
            jax.ShapeDtypeStruct((share, 2 * kw), jnp.bfloat16),
        ),
        [SM, VM, VM], 0, 3 * rows * width * 2, (place, tokens, norm_gain.reshape(1, width)), name="normed",
    )
    cross = swap(a_far[:, kw:], NEAR)
    near_share = swap(a_far[:, :kw], NEAR)
    cross = [cross] + [swap_rep(cross, far) for far in range(1, n_rep)]
    near_share = [near_share] + [swap_rep(near_share, far) for far in range(1, n_rep)]

    middle = HEAD_SIZE // 2
    exponent = jnp.arange(middle, dtype=jnp.float32) * (2.0 / HEAD_SIZE)
    starts = jnp.stack([(ctx ^ e) * rows for e in GROUP])
    positions = (starts[:, None] + jnp.arange(rows, dtype=jnp.int32)[None, :]).reshape(-1).astype(jnp.float32)
    angles = positions[:, None] * (ROPE_BASE ** (-exponent))[None, :]
    cosine, sine = jnp.cos(angles), jnp.sin(angles)
    cosine = jnp.concatenate([cosine, cosine], axis=1)
    sine = jnp.concatenate([-sine, sine], axis=1)

    kv_cols = kv_weight.shape[1]
    kv_blocks = weights("kv")
    kv_blocks += [swap(w, CORE) for w in kv_blocks]
    kept, sent = call(
        functools.partial(kv_body, n_rep),
        (
            jax.ShapeDtypeStruct((2 * rows, kv_cols), jnp.float32),
            jax.ShapeDtypeStruct((2 * rows, kv_cols), jnp.bfloat16),
        ),
        [SM] + [VM] * (2 + 2 * n_rep + 2 * n_masks), 8 * rows * kw * kv_cols, 4 * kw * (2 * rows + kv_cols),
        (place, a_own, a_core, *near_share, *cross, *kv_blocks), name="kv_project",
    )
    spread = local_heads // 2 // head_group
    cache, kv_own = call(
        functools.partial(kv_finish_body, spread),
        (
            jax.ShapeDtypeStruct((2 * rows, 2 * HEAD_SIZE), jnp.bfloat16),
            jax.ShapeDtypeStruct((rows, kv_cols), jnp.bfloat16),
        ),
        [SM] + [VM] * 5, 0, 14 * rows * kv_cols,
        (place, kept, swap(sent, NEAR), kv_bias.reshape(1, kv_cols), cosine, sine), name="kv_finish",
    )
    all_heads = gather_rep(kv_own, 1)
    ordered = []
    for v in range(2):
        for h in range(KEY_VALUE_HEADS):
            owner = h // kv_heads * (n_rep * kv_heads // KEY_VALUE_HEADS)
            first = owner * kv_cols + (v * kv_heads + h % kv_heads) * HEAD_SIZE
            ordered.append(all_heads[:, first : first + HEAD_SIZE])
    key_value_cache = jnp.concatenate(ordered, axis=1)
    (joined,) = call(
        functools.partial(join_body, n_rep), (jax.ShapeDtypeStruct((4 * rows, kw), jnp.bfloat16),),
        [SM] + [VM] * (2 + 2 * n_rep), 0, 16 * rows * kw,
        (place, a_own, swap(a_core, CORE), *near_share, *[swap(x, CORE) for x in cross]), name="joined",
    )
    near = (ctx >> 2) & 1

    rest("q2")
    came = []
    for bit in high_bits:
        came.append((cache, z_stream.swap(cache, bit)))
        cache = jnp.concatenate([cache, came[-1][1].v], axis=0)
    step("q3")
    cache = jnp.concatenate([came[-1][0], came[-1][1].v], axis=0)
    other = y_stream.swap(cache, Y)
    rest("q3")
    for i in range(n_out):
        step(f"o{i}")
        rest(f"o{i}")
    cache = jnp.concatenate([cache, other.v], axis=0)
    cache = jnp.concatenate([cache, swap(cache, CORE)], axis=0)

    n_tokens = rows * n_ctx
    own_bias = lax.dynamic_index_in_dim(bias, near * 2 + (ctx & 1), 0, keepdims=False)
    att = {d: [] for d in GROUP}
    for i in range(n_q):
        kept, sent = call(
            query_body,
            (
                jax.ShapeDtypeStruct((4 * rows, 2 * n), jnp.float32),
                jax.ShapeDtypeStruct((4 * rows, 2 * n), jnp.bfloat16),
            ),
            [SM] + [VM] * (1 + n_masks), 8 * rows * kw * 4 * n, 2 * kw * (4 * rows + 4 * n),
            (place, joined, *weights(f"q{i}")), name=f"q_project{i}",
        )
        mine, sent = call(
            halve_body,
            (jax.ShapeDtypeStruct((4 * rows, n), jnp.float32), jax.ShapeDtypeStruct((4 * rows, n), jnp.bfloat16)),
            [SM, VM, VM], 0, 4 * rows * n * 18, (place, kept, swap(sent, CORE)), name=f"q_halve{i}",
        )
        (attended,) = call(
            functools.partial(attend_body, n_bits),
            (jax.ShapeDtypeStruct((4 * rows, n), jnp.bfloat16),),
            [SM] + [VM] * 6, 4 * heads * 4 * rows * n_tokens * HEAD_SIZE * 2, 2 * n_tokens * HEAD_SIZE * 2,
            (place, mine, swap(sent, NEAR), own_bias[i : i + 1], cosine, sine, cache),
            scratch=[
                pltpu.VMEM((4 * heads * rows, HEAD_SIZE), jnp.bfloat16),
                pltpu.VMEM((4 * heads * rows, 2 * HEAD_SIZE), jnp.float32),
                pltpu.VMEM((4 * heads * rows, HEAD_SIZE), jnp.float32),
            ],
            name=f"attend{i}",
        )
        far = swap(attended, NEAR)
        att[0].append(attended)
        att[NEAR].append(far)
        att[CORE].append(swap(attended, CORE))
        att[NEAR | CORE].append(swap(far, CORE))
    size = rows // n_rep
    (collected,) = call(
        functools.partial(collect_body, n_q, heads),
        (jax.ShapeDtypeStruct((n_rep, 4 * size, local_heads * HEAD_SIZE), jnp.bfloat16),),
        [SM] + [VM] * (4 * n_q), 0, 16 * rows * local_heads * HEAD_SIZE,
        (place, *[a for d in GROUP for a in att[d]]), name="collected",
    )

    sums, fars, cores, crosses = [], [], [], []
    for s in range(n_out):
        cols = out_cols * n_masks
        (partial,) = call(
            output_body,
            (jax.ShapeDtypeStruct((n_rep, 4 * size, cols), jnp.bfloat16),),
            [VM] * (1 + n_masks), 8 * rows * out_weight.shape[0] * cols,
            2 * out_weight.shape[0] * (4 * rows + cols) + 8 * rows * cols,
            (collected, *weights(f"o{s}")), name=f"out_project{s}",
        )
        total = partial[0].astype(jnp.float32)
        for far in range(1, n_rep):
            total = total + swap_rep(partial[far], far).astype(jnp.float32)
        total = total.astype(jnp.bfloat16)
        came = swap(total[2 * size :], NEAR)
        sums.append(total)
        fars.append(came)
        cores.append(swap(total[size : 2 * size], CORE))
        crosses.append(swap(came[size:], CORE))
    (result,) = call(
        functools.partial(place_body, masks, n_out),
        (jax.ShapeDtypeStruct((size, width), jnp.bfloat16),),
        [SM] + [VM] * (4 * n_out), 0, 2 * size * width * 2, (place, *sums, *fars, *cores, *crosses), name="placed",
    )
    return result, key_value_cache


def solution(mesh):
    in_specs = (
        P("ctx", None),
        P(),
        P("ctx", "rep"),
        P("rep"),
        P("ctx", "rep"),
        P("rep"),
        P("rep", "ctx"),
    )
    out_specs = (P(("ctx", "rep"), None), P("ctx", None))
    return jax.shard_map(per_device, mesh=mesh, in_specs=in_specs, out_specs=out_specs, check_vma=False)
```
